32 devices in a mesh: groups: 2 (over y), ctx: 4 (over z), head: 2 (over x), role: 2 (over core).
Axes of the slice: x: 2, y: 2, z: 4, core: 2. Of those that a mesh axis runs over, the one named last changes fastest.
Arguments:
- prompt_query: bfloat16 [768, 64, 192], P(('groups', 'ctx'), ('head', 'role')), parts along dimension 0, may hold values from -200 to 200
- prompt_latent: bfloat16 [768, 576], P(('groups', 'ctx')), parts along dimension 0, may hold values from -60 to 60
- block_order: int32 [8], P('groups'), parts along dimension 0, may hold values from 0 to 3, as said below
- key_up: bfloat16 [64, 128, 512], P(('head', 'role')), may hold values from -0.5 to 0.5
- value_up: bfloat16 [64, 512, 128], P(('head', 'role')), may hold values from -1.796875 to 1.796875
- out_weight: bfloat16 [8192, 7168], P(('head', 'role'), 'ctx'), may hold values from -0.0625 to 0.0625
- step_query: bfloat16 [4, 8, 64, 192], P(None, 'groups', ('head', 'role')), parts along dimension 1, may hold values from -200 to 200
- cache_latent: bfloat16 [8, 1536, 576], P('groups', 'ctx'), parts along dimension 0, may hold values from -60 to 60
- step_latent: bfloat16 [4, 8, 576], P(None, 'groups'), parts along dimension 1, may hold values from -5 to 5
- cache_length: int32 [8], P('groups'), parts along dimension 0, may hold values from 2 to 1536
- block_dest: int32 [8], P('groups'), parts along dimension 0, may hold values from 0 to 3
Outputs:
- prompt_out: bfloat16 [768, 8192], P(('groups', 'ctx'), ('head', 'role')), parts along dimension 0
- step_out: bfloat16 [4, 8, 7168], P(None, 'groups', ('ctx', 'head', 'role')), parts along dimension 1
The draws below stay inside these ranges and needn't reach their ends.
There are 2 independent parts, one for each index of `groups`. The reference program is written for one: setup_inputs(seed, part) draws one part's arguments, and reference() takes and returns one part's arrays. A program takes and returns all parts, laid end to end along the dimension named above; an argument that names none is the same for every part. Nothing has to cross between parts.
Inputs may be any that keep to these rules, and one draw needn't show every extreme that they name: `block_order`: a permutation: each block position appears once.
All inputs are finite; a program needn't handle non-finite values.
Results may differ from the reference program's by a relative error of at most 0.039.
Values may be sent and summed in bfloat16 or wider, within the bound.
A program may use at most 64 MiB of HBM per device.

```python
import jax
import jax.numpy as jnp
from jax import lax

HEADS = 64
NOPE = 128
ROPE = 64
LATENT = 512
VDIM = 128
DMODEL = 7168
STEPS = 4
ROWS = 4
TOK_DEV = 96
SEQ = 384
CACHE = 1536
N_CTX = 4


def prompt_order(key):
    return jax.random.permutation(jax.random.fold_in(key, 101), N_CTX).astype(jnp.int32)


def prompt_keys(key):
    values = jnp.clip(jax.random.normal(jax.random.fold_in(key, 102), (SEQ, LATENT + ROPE), jnp.float32), -5.0, 5.0)
    return values


def cache_keys(key):
    values = jnp.clip(jax.random.normal(jax.random.fold_in(key, 202), (ROWS, CACHE, LATENT + ROPE), jnp.float32), -5.0, 5.0)
    return values


def draw_block_order(key, part):
    return prompt_order(key)


def draw_prompt_latent(key, part):
    return prompt_keys(key).astype(jnp.bfloat16)


def draw_cache_latent(key, part):
    return cache_keys(key).astype(jnp.bfloat16)


def draw_prompt_query(key, part):
    values = jnp.clip(jax.random.normal(jax.random.fold_in(key, 104), (SEQ, HEADS, NOPE + ROPE), jnp.float32), -5.0, 5.0)
    return values.astype(jnp.bfloat16)


def draw_step_query(key, part):
    values = jnp.clip(jax.random.normal(jax.random.fold_in(key, 204), (STEPS, ROWS, HEADS, NOPE + ROPE), jnp.float32), -5.0, 5.0)
    return values.astype(jnp.bfloat16)


def set_ends(drawn, key, least, largest):
    longest = drawn.shape.index(max(drawn.shape))
    spots = []
    for shift in (0, 1):
        where = [jax.random.randint(jax.random.fold_in(key, axis), (), 0, length) for axis, length in enumerate(drawn.shape)]
        where[longest] = (where[longest] + shift) % drawn.shape[longest]
        spots.append(tuple(where))
    return drawn.at[spots[0]].set(least).at[spots[1]].set(largest)


def block_scale(key, dims, pieces, smallest, high):
    gain = 1.0
    for dim, parts in pieces:
        draws = jax.random.uniform(jax.random.fold_in(jax.random.fold_in(key, 6), dim), (parts,), jnp.float32, smallest / len(pieces), high / len(pieces))
        gain = gain * jnp.repeat(jnp.exp(draws), dims[dim] // parts).reshape((-1,) + (1,) * (len(dims) - 1 - dim))
    return gain


def normal_values(rng, extent, spread, bound, shards=(), kind=jnp.bfloat16):
    gain = block_scale(rng, extent, shards, -0.22, 0.18) if shards else 1.0
    result = jax.random.normal(rng, extent, jnp.float32) * spread * gain
    return jnp.minimum(jnp.maximum(result, -bound), bound).astype(kind)


def setup_inputs(seed: int = 0, part: int = 0) -> dict:
    keys = jax.random.split(jax.random.key(seed), 12)
    part_keys = jax.random.split(jax.random.fold_in(keys[11], part), 12)
    return {
        "prompt_query": draw_prompt_query(jax.random.fold_in(jax.random.fold_in(keys[11], part), 71), part),
        "prompt_latent": draw_prompt_latent(jax.random.fold_in(jax.random.fold_in(keys[11], part), 71), part),
        "block_order": draw_block_order(jax.random.fold_in(jax.random.fold_in(keys[11], part), 71), part),
        "key_up": normal_values(keys[3], (HEADS, NOPE, LATENT), NOPE ** -0.5, 0.5, ((0, 4),)),
        "value_up": normal_values(keys[4], (HEADS, LATENT, VDIM), 0.3, 1.796875, ((0, 4),)),
        "out_weight": normal_values(keys[5], (HEADS * VDIM, DMODEL), (HEADS * VDIM) ** -0.5, 0.0625, ((0, 4), (1, 4))),
        "step_query": draw_step_query(jax.random.fold_in(jax.random.fold_in(keys[11], part), 71), part),
        "cache_latent": draw_cache_latent(jax.random.fold_in(jax.random.fold_in(keys[11], part), 71), part),
        "step_latent": normal_values(part_keys[8], (STEPS, ROWS, LATENT + ROPE), 1.0, 5.0),
        "cache_length": set_ends(jax.random.randint(part_keys[9], (ROWS,), 2, CACHE + 1), jax.random.fold_in(part_keys[9], 1), 2, CACHE).astype(jnp.int32),
        "block_dest": set_ends(jax.random.randint(part_keys[10], (N_CTX,), 0, ROWS), jax.random.fold_in(part_keys[10], 1), 0, ROWS - 1).astype(jnp.int32),
    }


def absorbed(queries, key_up):
    latent_part = jnp.einsum('...hn,hnc->...hc', queries[..., :NOPE].astype(jnp.float32), key_up.astype(jnp.float32)).astype(jnp.bfloat16)
    return jnp.concatenate([latent_part, queries[..., NOPE:]], axis=-1)


def reference(prompt_query, prompt_latent, block_order, key_up, value_up, out_weight, step_query, cache_latent, step_latent, cache_length, block_dest):
    score_scale = (NOPE + ROPE) ** -0.5
    position = (block_order[:, None] * TOK_DEV + jnp.arange(TOK_DEV, dtype=jnp.int32)[None, :]).reshape(SEQ).astype(jnp.int32)
    prompt_rows = absorbed(prompt_query, key_up)
    visible = position[None, :] <= position[:, None]

    def one_head(inputs):
        head_rows, head_value = inputs
        scores = jnp.dot(head_rows, prompt_latent.T, preferred_element_type=jnp.float32) * score_scale
        scores = jnp.where(visible, scores, jnp.float32(-1e30))
        highest = jnp.max(scores, axis=1)
        weights = jnp.where(visible, jnp.exp(scores - highest[:, None]), jnp.float32(0.0))
        totals = jnp.sum(weights, axis=1)
        summed = jnp.dot(weights.astype(jnp.bfloat16), prompt_latent[:, :LATENT], preferred_element_type=jnp.float32)
        attended = (summed / totals[:, None]).astype(jnp.bfloat16)
        return jnp.dot(attended, head_value, preferred_element_type=jnp.float32).astype(jnp.bfloat16)

    head_outs = lax.map(one_head, (jnp.transpose(prompt_rows, (1, 0, 2)), value_up))
    prompt_out = jnp.transpose(head_outs, (1, 0, 2)).reshape(SEQ, HEADS * VDIM)

    step_rows = absorbed(step_query, key_up).astype(jnp.float32)
    cache_scores = jnp.einsum('sbhc,bpc->sbhp', step_rows, cache_latent.astype(jnp.float32)) * score_scale
    live_mask = (jnp.arange(CACHE, dtype=jnp.int32)[None, :] < cache_length[:, None])[None, :, None, :]
    cache_scores = jnp.where(live_mask, cache_scores, jnp.float32(-1e30))
    token_block = (jnp.arange(SEQ, dtype=jnp.int32) // TOK_DEV).astype(jnp.int32)
    handed = (block_dest[token_block][None, :] == jnp.arange(ROWS, dtype=jnp.int32)[:, None])[None, :, None, :]
    handed_scores = jnp.einsum('sbhc,jc->sbhj', step_rows, prompt_latent.astype(jnp.float32)) * score_scale
    handed_scores = jnp.where(handed, handed_scores, jnp.float32(-1e30))
    fresh_scores = jnp.einsum('sbhc,ubc->sbhu', step_rows, step_latent.astype(jnp.float32)) * score_scale
    step_ids = jnp.arange(STEPS, dtype=jnp.int32)
    order_mask = (step_ids[None, :] <= step_ids[:, None])[:, None, None, :]
    fresh_scores = jnp.where(order_mask, fresh_scores, jnp.float32(-1e30))
    highest = jnp.maximum(jnp.maximum(jnp.max(cache_scores, axis=-1), jnp.max(fresh_scores, axis=-1)), jnp.max(handed_scores, axis=-1))
    cache_weights = jnp.where(live_mask, jnp.exp(cache_scores - highest[..., None]), jnp.float32(0.0))
    handed_weights = jnp.where(handed, jnp.exp(handed_scores - highest[..., None]), jnp.float32(0.0))
    fresh_weights = jnp.where(order_mask, jnp.exp(fresh_scores - highest[..., None]), jnp.float32(0.0))
    totals = jnp.sum(cache_weights, axis=-1) + jnp.sum(handed_weights, axis=-1) + jnp.sum(fresh_weights, axis=-1)
    summed = jnp.einsum('sbhp,bpc->sbhc', cache_weights.astype(jnp.bfloat16).astype(jnp.float32), cache_latent[..., :LATENT].astype(jnp.float32))
    summed = summed + jnp.einsum('sbhj,jc->sbhc', handed_weights.astype(jnp.bfloat16).astype(jnp.float32), prompt_latent[:, :LATENT].astype(jnp.float32))
    summed = summed + jnp.einsum('sbhu,ubc->sbhc', fresh_weights.astype(jnp.bfloat16).astype(jnp.float32), step_latent[..., :LATENT].astype(jnp.float32))
    attended = (summed / totals[..., None]).astype(jnp.bfloat16)
    step_heads = jnp.einsum('sbhc,hcv->sbhv', attended.astype(jnp.float32), value_up.astype(jnp.float32)).astype(jnp.bfloat16)
    step_heads = step_heads.reshape(STEPS * ROWS, HEADS * VDIM)
    step_out = jnp.dot(step_heads, out_weight, preferred_element_type=jnp.float32).astype(jnp.bfloat16).reshape(STEPS, ROWS, DMODEL)
    return prompt_out, step_out
```

```python
import functools
import math

import jax
import jax.numpy as jnp
from jax import lax
from jax.experimental import pallas as pl
from jax.experimental.pallas import tpu as pltpu
from jax.sharding import PartitionSpec as P

MESH = pl.DeviceIdType.MESH
LOW = -1e30


def nt_dot(a, b):
    return lax.dot_general(a, b, (((1,), (1,)), ((), ())), preferred_element_type=jnp.float32)


def nn_dot(a, b):
    return jnp.dot(a, b, preferred_element_type=jnp.float32)


def head_major(rows, heads):
    out_row = lax.broadcasted_iota(jnp.int32, (rows * heads, rows * heads), 0)
    in_row = lax.broadcasted_iota(jnp.int32, (rows * heads, rows * heads), 1)
    wanted = lax.rem(out_row, rows) * heads + lax.div(out_row, rows)
    return (in_row == wanted).astype(jnp.bfloat16)


def kernel(
    size,
    order_ref, length_ref, dest_ref,
    pq_hbm, pl_hbm, ku_hbm, vu_hbm, ow_hbm, sq_hbm, cache_hbm, sl_ref,
    prompt_ref, step_ref,
    pq, ku, vu, ow, sq, cache, own, keys, query, absorbed, step_rows, sums, stats, partials, flat, parts, landed,
    local_sem, lat_send, lat_recv, fwd_send, fwd_recv, part_send, part_recv, stat_send, stat_recv, out_send, out_recv,
):
    n_ctx, n_head, n_role = size["ctx"], size["head"], size["role"]
    plane = n_head * n_role
    tokens, heads, nope, latent = size["tokens"], size["heads"], size["nope"], size["latent"]
    steps, rows, span, vdim = size["steps"], size["rows"], size["span"], size["vdim"]
    made = steps * rows
    half = tokens // n_role
    scale = (size["width"] ** -0.5) * math.log2(math.e)
    place, role = lax.axis_index("ctx"), lax.axis_index("role")
    here = lax.axis_index("head") * n_role + role

    def ctx_peer(k):
        return {"ctx": lax.rem(place + k, n_ctx)}

    def plane_peer(k):
        other = lax.rem(here + k, plane)
        return {"head": lax.div(other, n_role), "role": lax.rem(other, n_role)}

    def load(i, src, dst):
        copy = pltpu.make_async_copy(src, dst, local_sem.at[i])
        copy.start()
        return copy

    sq_copy = load(0, sq_hbm, sq)
    pq_copy = load(1, pq_hbm, pq)
    ku_copy = load(2, ku_hbm, ku)
    own_copy = load(3, pl_hbm, own)
    cache_copy = load(4, cache_hbm, cache)
    keys_copy = load(5, pl_hbm, keys.at[pl.ds(pl.multiple_of(place * tokens, 16), tokens)])

    barrier = pltpu.get_barrier_semaphore()
    for k in range(1, n_ctx):
        pl.semaphore_signal(barrier, inc=1, device_id=ctx_peer(k), device_id_type=MESH)
    for k in range(1, plane):
        pl.semaphore_signal(barrier, inc=1, device_id=plane_peer(k), device_id_type=MESH)
    pl.semaphore_wait(barrier, n_ctx - 1 + plane - 1)

    my_half = pl.multiple_of(role * half, 16)
    lat_copies = []
    for k in range(1, n_ctx):
        copy = pltpu.make_async_remote_copy(
            src_ref=pl_hbm.at[pl.ds(my_half, half)],
            dst_ref=keys.at[pl.ds(pl.multiple_of(place * tokens + role * half, 16), half)],
            send_sem=lat_send.at[k], recv_sem=lat_recv.at[k],
            device_id=ctx_peer(k), device_id_type=MESH,
        )
        copy.start()
        lat_copies.append(copy)
    vu_copy = load(6, vu_hbm, vu)
    ow_copy = load(7, ow_hbm, ow)

    total = tokens + made
    sq_copy.wait()
    step_perm = head_major(made, heads)
    query[:, tokens:, :] = nn_dot(step_perm, sq[...]).astype(jnp.bfloat16).reshape(heads, made, size["width"])
    pq_copy.wait()
    tile = 16
    perm = step_perm if made == tile else head_major(tile, heads)
    for i in range(tokens // tile):
        moved = nn_dot(perm, pq[i * tile * heads : (i + 1) * tile * heads, :]).astype(jnp.bfloat16)
        query[:, i * tile : (i + 1) * tile, :] = moved.reshape(heads, tile, size["width"])
    ku_copy.wait()
    for h in range(heads):
        low = nn_dot(query[h, :, :nope], ku[h]).astype(jnp.bfloat16)
        absorbed[h * tokens : (h + 1) * tokens, :latent] = low[:tokens]
        absorbed[h * tokens : (h + 1) * tokens, latent:] = query[h, :tokens, nope:]
        step_rows[h * made : (h + 1) * made, :latent] = low[tokens:]
        step_rows[h * made : (h + 1) * made, latent:] = query[h, tokens:, nope:]

    count = heads * made
    row_id = lax.rem(lax.broadcasted_iota(jnp.int32, (count, 1), 0), made)
    row_step, row_request = lax.div(row_id, rows), lax.rem(row_id, rows)
    step_q = step_rows[...]
    fresh = jnp.concatenate([sl_ref[u].astype(jnp.float32) for u in range(steps)], axis=0).astype(jnp.bfloat16)
    fresh_id = lax.broadcasted_iota(jnp.int32, (1, made), 1)
    fresh_mask = (lax.rem(fresh_id, rows) == row_request) & (lax.div(fresh_id, rows) <= row_step) & (place == 0)
    scores = [jnp.where(fresh_mask, nt_dot(step_q, fresh) * scale, LOW)]
    values = [fresh[:, :latent]]
    own_copy.wait()
    handed = row_request == dest_ref[place]
    scores.append(jnp.where(handed, nt_dot(step_q, own[...]) * scale, LOW))
    values.append(own[:, :latent])
    cache_copy.wait()
    cache_pos = place * span + lax.broadcasted_iota(jnp.int32, (1, span), 1)
    for b in range(rows):
        live = (cache_pos < length_ref[b]) & (row_request == b)
        scores.append(jnp.where(live, nt_dot(step_q, cache[b]) * scale, LOW))
        values.append(cache[b, :, :latent])
    peak = functools.reduce(jnp.maximum, [jnp.max(s, axis=1, keepdims=True) for s in scores])
    amount = jnp.zeros((count, 1), jnp.float32)
    summed = jnp.zeros((count, latent), jnp.float32)
    for s, v in zip(scores, values):
        w = jnp.exp2(s - peak)
        amount = amount + jnp.sum(w, axis=1, keepdims=True)
        summed = summed + nn_dot(w.astype(jnp.bfloat16), v)
    sums[...] = summed.astype(jnp.bfloat16)
    lane = lax.broadcasted_iota(jnp.int32, (made, 128), 1)
    peaks = jnp.full((made, 128), 0.0, jnp.float32)
    amounts = jnp.full((made, 128), 1.0, jnp.float32)
    for h in range(heads):
        peaks = jnp.where(lane == h, peak[h * made : (h + 1) * made], peaks)
        amounts = jnp.where(lane == h, amount[h * made : (h + 1) * made], amounts)
    stats[0, :made] = peaks
    stats[0, made:] = amounts
    vu_copy.wait()
    for h in range(heads):
        partials[0, :, h * vdim : (h + 1) * vdim] = nn_dot(
            sums[h * made : (h + 1) * made, :], vu[h]
        ).astype(jnp.bfloat16)
    part_copies = []
    for k in range(1, n_ctx):
        for src, send, recv in ((stats, stat_send, stat_recv), (partials, part_send, part_recv)):
            copy = pltpu.make_async_remote_copy(
                src_ref=src.at[0], dst_ref=src.at[k], send_sem=send.at[k], recv_sem=recv.at[k],
                device_id=ctx_peer(k), device_id_type=MESH,
            )
            copy.start()
            part_copies.append(copy)

    fwd_copies = []
    for k in range(1, n_ctx):
        lat_copies[k - 1].wait_recv()
        source = lax.rem(place + n_ctx - k, n_ctx)
        piece = keys.at[pl.ds(pl.multiple_of(source * tokens + role * half, 16), half)]
        for j in range(1, n_role):
            copy = pltpu.make_async_remote_copy(
                src_ref=piece, dst_ref=piece, send_sem=fwd_send.at[k, j], recv_sem=fwd_recv.at[k, j],
                device_id={"role": lax.rem(role + j, n_role)}, device_id_type=MESH,
            )
            copy.start()
            fwd_copies.append(copy)

    keys_copy.wait()
    for copy in fwd_copies:
        copy.wait_recv()
    seq = n_ctx * tokens
    key_id = lax.broadcasted_iota(jnp.int32, (1, seq), 1)
    key_pos = jnp.zeros((1, seq), jnp.int32)
    for k in range(n_ctx):
        inside = (key_id >= k * tokens) & (key_id < (k + 1) * tokens)
        key_pos = jnp.where(inside, order_ref[k] * tokens + key_id - k * tokens, key_pos)
    query_pos = order_ref[place] * tokens + lax.broadcasted_iota(jnp.int32, (tokens, 1), 0)
    bias = jnp.where(key_pos <= query_pos, 0.0, LOW).astype(jnp.float32)
    group = size["group"]

    def prompt_group(g):
        at = g * group * tokens
        s = nt_dot(absorbed[at : at + group * tokens, :], keys[...]) * scale
        s = s.reshape(group, tokens, seq) + bias[None]
        w = jnp.exp2(s - jnp.max(s, axis=2, keepdims=True))
        inverse = 1.0 / jnp.sum(w, axis=2, keepdims=True)
        o = nn_dot(w.astype(jnp.bfloat16).reshape(group * tokens, seq), keys[:, :latent])
        attended = (o.reshape(group, tokens, latent) * inverse).astype(jnp.bfloat16)
        for i in range(group):
            h = g * group + i
            prompt_ref[:, h * vdim : (h + 1) * vdim] = nn_dot(attended[i], vu[h]).astype(jnp.bfloat16)

    n_groups = heads // group
    first = n_groups // 2
    for g in range(first):
        prompt_group(g)

    for copy in part_copies:
        copy.wait_recv()
    top = stats[0, :made]
    for k in range(1, n_ctx):
        top = jnp.maximum(top, stats[k, :made])
    factors = [jnp.exp2(stats[k, :made] - top) for k in range(n_ctx)]
    whole = functools.reduce(jnp.add, [factors[k] * stats[k, made:] for k in range(n_ctx)])
    factors = [f / whole for f in factors]
    for h in range(heads):
        cols = slice(h * vdim, (h + 1) * vdim)
        merged = functools.reduce(
            jnp.add, [partials[k, :, cols].astype(jnp.float32) * factors[k][:, h : h + 1] for k in range(n_ctx)]
        )
        flat[:, cols] = merged.astype(jnp.bfloat16)
    ow_copy.wait()
    projected = nn_dot(flat[...], ow[...])
    width = projected.shape[1] // plane
    for d in range(plane):
        parts[d] = projected[:, d * width : (d + 1) * width]
    out_copies = []
    for k in range(1, plane):
        copy = pltpu.make_async_remote_copy(
            src_ref=parts.at[lax.rem(here + k, plane)], dst_ref=landed.at[k],
            send_sem=out_send.at[k], recv_sem=out_recv.at[k],
            device_id=plane_peer(k), device_id_type=MESH,
        )
        copy.start()
        out_copies.append(copy)

    for g in range(first, n_groups):
        prompt_group(g)

    result = parts[here]
    for k in range(1, plane):
        out_copies[k - 1].wait_recv()
        result = result + landed[k]
    step_ref[...] = result.astype(jnp.bfloat16)
    for copy in lat_copies + fwd_copies + part_copies + out_copies:
        copy.wait_send()


def per_device(
    prompt_query, prompt_latent, block_order, key_up, value_up, out_weight,
    step_query, cache_latent, step_latent, cache_length, block_dest,
):
    tokens, heads, width = prompt_query.shape
    nope, latent = key_up.shape[1:]
    vdim = value_up.shape[2]
    steps, rows = step_query.shape[:2]
    span, key_width = cache_latent.shape[1:]
    model = out_weight.shape[1]
    n_ctx, n_head, n_role = (lax.axis_size(a) for a in ("ctx", "head", "role"))
    plane, made, seq = n_head * n_role, steps * rows, n_ctx * tokens
    group = 4 if heads % 4 == 0 and seq <= 512 else 1
    size = dict(
        ctx=n_ctx, head=n_head, role=n_role, tokens=tokens, heads=heads, width=width, nope=nope,
        latent=latent, vdim=vdim, steps=steps, rows=rows, span=span, group=group,
    )
    bf16, f32 = jnp.bfloat16, jnp.float32
    smem, anywhere, vmem = (pl.BlockSpec(memory_space=m) for m in (pltpu.SMEM, pl.ANY, pltpu.VMEM))
    dma = pltpu.SemaphoreType.DMA
    prompt_out, step_out = pl.pallas_call(
        functools.partial(kernel, size),
        out_shape=(
            jax.ShapeDtypeStruct((tokens, heads * vdim), bf16),
            jax.ShapeDtypeStruct((made, model // plane), bf16),
        ),
        in_specs=[smem] * 3 + [anywhere] * 7 + [vmem],
        out_specs=(vmem, vmem),
        scratch_shapes=[
            pltpu.VMEM((tokens * heads, width), bf16),
            pltpu.VMEM(key_up.shape, bf16),
            pltpu.VMEM(value_up.shape, bf16),
            pltpu.VMEM(out_weight.shape, bf16),
            pltpu.VMEM((made * heads, width), bf16),
            pltpu.VMEM(cache_latent.shape, bf16),
            pltpu.VMEM((tokens, key_width), bf16),
            pltpu.VMEM((seq, key_width), bf16),
            pltpu.VMEM((heads, tokens + made, width), bf16),
            pltpu.VMEM((heads * tokens, key_width), bf16),
            pltpu.VMEM((heads * made, key_width), bf16),
            pltpu.VMEM((heads * made, latent), bf16),
            pltpu.VMEM((n_ctx, 2 * made, 128), f32),
            pltpu.VMEM((n_ctx, made, heads * vdim), bf16),
            pltpu.VMEM((made, heads * vdim), bf16),
            pltpu.VMEM((plane, made, model // plane), f32),
            pltpu.VMEM((plane, made, model // plane), f32),
            dma((8,)),
            dma((n_ctx,)), dma((n_ctx,)),
            dma((n_ctx, n_role)), dma((n_ctx, n_role)),
            dma((n_ctx,)), dma((n_ctx,)),
            dma((n_ctx,)), dma((n_ctx,)),
            dma((plane,)), dma((plane,)),
        ],
        compiler_params=pltpu.CompilerParams(
            collective_id=0, has_side_effects=True, vmem_limit_bytes=56 * 1024 * 1024
        ),
    )(
        block_order, cache_length, block_dest,
        prompt_query.reshape(tokens * heads, width), prompt_latent, key_up, value_up, out_weight,
        step_query.reshape(made * heads, width), cache_latent, step_latent,
    )
    return prompt_out, step_out.reshape(steps, rows, model // plane)


def solution(mesh):
    return jax.shard_map(
        per_device,
        mesh=mesh,
        in_specs=(
            P(("groups", "ctx"), ("head", "role"), None),
            P(("groups", "ctx"), None),
            P("groups"),
            P(("head", "role"), None, None),
            P(("head", "role"), None, None),
            P(("head", "role"), "ctx"),
            P(None, "groups", ("head", "role"), None),
            P("groups", "ctx", None),
            P(None, "groups", None),
            P("groups"),
            P("groups"),
        ),
        out_specs=(
            P(("groups", "ctx"), ("head", "role")),
            P(None, "groups", ("ctx", "head", "role")),
        ),
        check_vma=False,
    )
```

```python
import functools
import math

import jax
import jax.numpy as jnp
from jax import lax
from jax.experimental import pallas as pl
from jax.experimental.pallas import tpu as pltpu
from jax.sharding import PartitionSpec as P

MESH = pl.DeviceIdType.MESH
LOW = -1e30


def nt_dot(a, b):
    return lax.dot_general(a, b, (((1,), (1,)), ((), ())), preferred_element_type=jnp.float32)


def nn_dot(a, b):
    return jnp.dot(a, b, preferred_element_type=jnp.float32)


def one_hot_rows(count, source):
    out_row = lax.broadcasted_iota(jnp.int32, (count, count), 0)
    in_row = lax.broadcasted_iota(jnp.int32, (count, count), 1)
    return (in_row == source(out_row)).astype(jnp.bfloat16)


def kernel(
    size,
    order_ref, length_ref, dest_ref,
    pq_hbm, pl_hbm, ku_hbm, vu_hbm, ow_hbm, sq_hbm, cache_hbm, sl_ref,
    prompt_hbm, step_ref,
    pq, ku, vu, ow, sq, cache, own, keys, query, absorbed, step_rows, sums, stats, partials, flat, parts, landed,
    prompt, prompt_sem, local_sem, lat_send, lat_recv, fwd_send, fwd_recv, part_send, part_recv, stat_send, stat_recv, out_send, out_recv,
):
    n_ctx, n_head, n_role = size["ctx"], size["head"], size["role"]
    plane = n_head * n_role
    tokens, heads, nope, latent = size["tokens"], size["heads"], size["nope"], size["latent"]
    steps, rows, span, vdim = size["steps"], size["rows"], size["span"], size["vdim"]
    made = steps * rows
    half = tokens // n_role
    scale = (size["width"] ** -0.5) * math.log2(math.e)
    place, role = lax.axis_index("ctx"), lax.axis_index("role")
    here = lax.axis_index("head") * n_role + role

    def ctx_peer(k):
        return {"ctx": lax.rem(place + k, n_ctx)}

    def plane_peer(k):
        other = lax.rem(here + k, plane)
        return {"head": lax.div(other, n_role), "role": lax.rem(other, n_role)}

    def load(i, src, dst):
        copy = pltpu.make_async_copy(src, dst, local_sem.at[i])
        copy.start()
        return copy

    sq_copy = load(0, sq_hbm, sq)
    pq_copy = load(1, pq_hbm, pq)
    ku_copy = load(2, ku_hbm, ku)
    own_copy = load(3, pl_hbm, own)
    cache_copy = load(4, cache_hbm, cache)
    keys_copy = load(5, pl_hbm, keys.at[pl.ds(pl.multiple_of(place * tokens, 16), tokens)])

    barrier = pltpu.get_barrier_semaphore()
    for k in range(1, n_ctx):
        pl.semaphore_signal(barrier, inc=1, device_id=ctx_peer(k), device_id_type=MESH)
    for k in range(1, plane):
        pl.semaphore_signal(barrier, inc=1, device_id=plane_peer(k), device_id_type=MESH)

    tile = 16

    def prompt_row(r):
        return lax.rem(r, tile) * heads + lax.div(r, tile)

    def step_row(r):
        within = lax.rem(r, made)
        return (lax.rem(within, steps) * rows + lax.div(within, steps)) * heads + lax.div(r, made)

    sq_copy.wait()
    moved = nn_dot(one_hot_rows(made * heads, step_row), sq[...]).astype(jnp.bfloat16)
    query[:, tokens:, :] = moved.reshape(heads, made, size["width"])
    perm = one_hot_rows(tile * heads, prompt_row)
    pq_copy.wait()
    for i in range(tokens // tile):
        moved = nn_dot(perm, pq[i * tile * heads : (i + 1) * tile * heads, :]).astype(jnp.bfloat16)
        query[:, i * tile : (i + 1) * tile, :] = moved.reshape(heads, tile, size["width"])

    pl.semaphore_wait(barrier, n_ctx - 1 + plane - 1)

    my_half = pl.multiple_of(role * half, 16)
    lat_copies = []
    for k in range(1, n_ctx):
        copy = pltpu.make_async_remote_copy(
            src_ref=pl_hbm.at[pl.ds(my_half, half)],
            dst_ref=keys.at[pl.ds(pl.multiple_of(place * tokens + role * half, 16), half)],
            send_sem=lat_send.at[k], recv_sem=lat_recv.at[k],
            device_id=ctx_peer(k), device_id_type=MESH,
        )
        copy.start()
        lat_copies.append(copy)
    vu_copy = load(6, vu_hbm, vu)
    ow_copy = load(7, ow_hbm, ow)

    ku_copy.wait()
    for h in range(heads):
        low = nn_dot(query[h, :, :nope], ku[h]).astype(jnp.bfloat16)
        absorbed[h * tokens : (h + 1) * tokens, :latent] = low[:tokens]
        absorbed[h * tokens : (h + 1) * tokens, latent:] = query[h, :tokens, nope:]
        step_low = low[tokens:].astype(jnp.float32)
        step_high = query[h, tokens:, nope:].astype(jnp.float32)
        for b in range(rows):
            step_rows[b, h * steps : (h + 1) * steps, :latent] = step_low[b * steps : (b + 1) * steps]
            step_rows[b, h * steps : (h + 1) * steps, latent:] = step_high[b * steps : (b + 1) * steps]

    each = heads * steps
    count = rows * each
    row_id = lax.broadcasted_iota(jnp.int32, (count, 1), 0)
    row_step, row_request = lax.rem(row_id, steps), lax.div(row_id, each)
    step_q = step_rows[...].astype(jnp.bfloat16)
    flat_q = step_q.reshape(count, step_q.shape[2])
    fresh = jnp.concatenate([sl_ref[u].astype(jnp.float32) for u in range(steps)], axis=0).astype(jnp.bfloat16)
    fresh_id = lax.broadcasted_iota(jnp.int32, (1, made), 1)
    fresh_mask = (lax.rem(fresh_id, rows) == row_request) & (lax.div(fresh_id, rows) <= row_step) & (place == 0)
    fresh_scores = jnp.where(fresh_mask, nt_dot(flat_q, fresh) * scale, LOW)
    own_copy.wait()
    own_scores = jnp.where(row_request == dest_ref[place], nt_dot(flat_q, own[...]) * scale, LOW)
    cache_copy.wait()
    cache_pos = place * span + lax.broadcasted_iota(jnp.int32, (1, span), 1)
    cache_scores = jnp.concatenate(
        [jnp.where(cache_pos < length_ref[b], nn_dot(step_q[b], cache[b]) * scale, LOW) for b in range(rows)], axis=0
    )
    peak = functools.reduce(
        jnp.maximum, [jnp.max(x, axis=1, keepdims=True) for x in (cache_scores, own_scores, fresh_scores)]
    )
    cache_w, own_w, fresh_w = (jnp.exp2(x - peak) for x in (cache_scores, own_scores, fresh_scores))
    amount = functools.reduce(jnp.add, [jnp.sum(x, axis=1, keepdims=True) for x in (cache_w, own_w, fresh_w)])
    cache_w = cache_w.astype(jnp.bfloat16)
    summed = nn_dot(own_w.astype(jnp.bfloat16), own[:, :latent]) + nn_dot(
        fresh_w.astype(jnp.bfloat16), fresh[:, :latent]
    )
    for b in range(rows):
        sums[b] = summed[b * each : (b + 1) * each] + nt_dot(
            cache_w[b * each : (b + 1) * each], cache[b, :latent, :]
        )
    lane = lax.broadcasted_iota(jnp.int32, (1, 128), 1)
    at_head = lane == lax.div(lax.rem(row_id, each), steps)

    def by_head(column, other):
        spread = jnp.where(at_head, column, 0.0).reshape(rows, each // 8, 8, 128).sum(axis=1)
        table = jnp.concatenate(
            [
                functools.reduce(jnp.add, [spread[b, j : j + steps] for j in range(0, 8, steps)])
                for b in range(rows)
            ],
            axis=0,
        )
        return jnp.where(lane < heads, table, other)

    stats[0, :made] = by_head(peak, 0.0)
    stats[0, made:] = by_head(amount, 1.0)
    vu_copy.wait()
    for h in range(heads):
        mine = jnp.concatenate([sums[b, h * steps : (h + 1) * steps, :] for b in range(rows)], axis=0)
        partials[0, :, h * vdim : (h + 1) * vdim] = nn_dot(mine.astype(jnp.bfloat16), vu[h]).astype(jnp.bfloat16)
    part_copies = []
    for k in range(1, n_ctx):
        for src, send, recv in ((stats, stat_send, stat_recv), (partials, part_send, part_recv)):
            copy = pltpu.make_async_remote_copy(
                src_ref=src.at[0], dst_ref=src.at[k], send_sem=send.at[k], recv_sem=recv.at[k],
                device_id=ctx_peer(k), device_id_type=MESH,
            )
            copy.start()
            part_copies.append(copy)

    fwd_copies = []
    for k in range(1, n_ctx):
        lat_copies[k - 1].wait_recv()
        source = lax.rem(place + n_ctx - k, n_ctx)
        piece = keys.at[pl.ds(pl.multiple_of(source * tokens + role * half, 16), half)]
        for j in range(1, n_role):
            copy = pltpu.make_async_remote_copy(
                src_ref=piece, dst_ref=piece, send_sem=fwd_send.at[k, j], recv_sem=fwd_recv.at[k, j],
                device_id={"role": lax.rem(role + j, n_role)}, device_id_type=MESH,
            )
            copy.start()
            fwd_copies.append(copy)

    keys_copy.wait()
    for copy in fwd_copies:
        copy.wait_recv()
    seq = n_ctx * tokens
    key_id = lax.broadcasted_iota(jnp.int32, (1, seq), 1)
    key_pos = jnp.zeros((1, seq), jnp.int32)
    for k in range(n_ctx):
        inside = (key_id >= k * tokens) & (key_id < (k + 1) * tokens)
        key_pos = jnp.where(inside, order_ref[k] * tokens + key_id - k * tokens, key_pos)
    query_pos = order_ref[place] * tokens + lax.broadcasted_iota(jnp.int32, (tokens, 1), 0)
    bias = jnp.where(key_pos <= query_pos, 0.0, LOW).astype(jnp.float32)
    group = size["group"]

    def prompt_scores(g):
        return nt_dot(absorbed[g * group * tokens : (g + 1) * group * tokens, :], keys[...])

    prompt_copies = []

    def prompt_finish(g, s):
        s = (s * scale).reshape(group, tokens, seq) + bias[None]
        w = jnp.exp2(s - jnp.max(s, axis=2, keepdims=True))
        inverse = 1.0 / jnp.sum(w, axis=2, keepdims=True)
        o = nn_dot(w.astype(jnp.bfloat16).reshape(group * tokens, seq), keys[:, :latent])
        attended = (o.reshape(group, tokens, latent) * inverse).astype(jnp.bfloat16)
        for i in range(group):
            h = g * group + i
            prompt[:, h * vdim : (h + 1) * vdim] = nn_dot(attended[i], vu[h]).astype(jnp.bfloat16)
        cols = slice(g * group * vdim, (g + 1) * group * vdim)
        copy = pltpu.make_async_copy(prompt.at[:, cols], prompt_hbm.at[:, cols], prompt_sem.at[g])
        copy.start()
        prompt_copies.append(copy)

    n_groups = heads // group
    first = n_groups // 2
    ahead = prompt_scores(0)
    for g in range(first):
        current, ahead = ahead, prompt_scores(g + 1)
        prompt_finish(g, current)

    for copy in part_copies:
        copy.wait_recv()
    top = stats[0, :made]
    for k in range(1, n_ctx):
        top = jnp.maximum(top, stats[k, :made])
    factors = [jnp.exp2(stats[k, :made] - top) for k in range(n_ctx)]
    whole = functools.reduce(jnp.add, [factors[k] * stats[k, made:] for k in range(n_ctx)])
    factors = [f / whole for f in factors]
    for h in range(heads):
        cols = slice(h * vdim, (h + 1) * vdim)
        merged = functools.reduce(
            jnp.add, [partials[k, :, cols].astype(jnp.float32) * factors[k][:, h : h + 1] for k in range(n_ctx)]
        )
        flat[:, cols] = merged.astype(jnp.bfloat16)
    ow_copy.wait()
    in_order = one_hot_rows(made, lambda r: lax.rem(r, rows) * steps + lax.div(r, rows))
    projected = nn_dot(nn_dot(in_order, flat[...]).astype(jnp.bfloat16), ow[...])
    width = projected.shape[1] // plane
    for d in range(plane):
        parts[d] = projected[:, d * width : (d + 1) * width]
    out_copies = []
    for k in range(1, plane):
        copy = pltpu.make_async_remote_copy(
            src_ref=parts.at[lax.rem(here + k, plane)], dst_ref=landed.at[k],
            send_sem=out_send.at[k], recv_sem=out_recv.at[k],
            device_id=plane_peer(k), device_id_type=MESH,
        )
        copy.start()
        out_copies.append(copy)

    for g in range(first, n_groups):
        current, ahead = ahead, prompt_scores(g + 1) if g + 1 < n_groups else None
        prompt_finish(g, current)

    result = parts[here]
    for k in range(1, plane):
        out_copies[k - 1].wait_recv()
        result = result + landed[k]
    step_ref[...] = result
    for copy in lat_copies + fwd_copies + part_copies + out_copies:
        copy.wait_send()
    for copy in prompt_copies:
        copy.wait()


def write_results(prompt_in, step_in, prompt_out, step_out, sem):
    copy = pltpu.make_async_copy(prompt_in, prompt_out, sem)
    copy.start()
    steps, rows = step_out.shape[:2]
    for t in range(steps):
        step_out[t] = step_in[t * rows : (t + 1) * rows, :].astype(step_out.dtype)
    copy.wait()


def per_device(
    prompt_query, prompt_latent, block_order, key_up, value_up, out_weight,
    step_query, cache_latent, step_latent, cache_length, block_dest,
):
    tokens, heads, width = prompt_query.shape
    nope, latent = key_up.shape[1:]
    vdim = value_up.shape[2]
    steps, rows = step_query.shape[:2]
    span, key_width = cache_latent.shape[1:]
    model = out_weight.shape[1]
    n_ctx, n_head, n_role = (lax.axis_size(a) for a in ("ctx", "head", "role"))
    plane, made, seq = n_head * n_role, steps * rows, n_ctx * tokens
    group = 4 if heads % 4 == 0 and seq <= 512 else 1
    size = dict(
        ctx=n_ctx, head=n_head, role=n_role, tokens=tokens, heads=heads, width=width, nope=nope,
        latent=latent, vdim=vdim, steps=steps, rows=rows, span=span, group=group,
    )
    bf16, f32 = jnp.bfloat16, jnp.float32
    smem, anywhere, vmem = (pl.BlockSpec(memory_space=m) for m in (pltpu.SMEM, pl.ANY, pltpu.VMEM))
    dma = pltpu.SemaphoreType.DMA
    prompt_made, step_made = pl.pallas_call(
        functools.partial(kernel, size),
        out_shape=(
            jax.ShapeDtypeStruct((tokens, heads * vdim), bf16),
            jax.ShapeDtypeStruct((made, model // plane), f32),
        ),
        in_specs=[smem] * 3 + [anywhere] * 7 + [vmem],
        out_specs=(anywhere, vmem),
        scratch_shapes=[
            pltpu.VMEM((tokens * heads, width), bf16),
            pltpu.VMEM(key_up.shape, bf16),
            pltpu.VMEM(value_up.shape, bf16),
            pltpu.VMEM(out_weight.shape, bf16),
            pltpu.VMEM((made * heads, width), bf16),
            pltpu.VMEM((rows, key_width, span), bf16),
            pltpu.VMEM((tokens, key_width), bf16),
            pltpu.VMEM((seq, key_width), bf16),
            pltpu.VMEM((heads, tokens + made, width), bf16),
            pltpu.VMEM((heads * tokens, key_width), bf16),
            pltpu.VMEM((rows, heads * steps, key_width), f32),
            pltpu.VMEM((rows, heads * steps, latent), f32),
            pltpu.VMEM((n_ctx, 2 * made, 128), f32),
            pltpu.VMEM((n_ctx, made, heads * vdim), bf16),
            pltpu.VMEM((made, heads * vdim), bf16),
            pltpu.VMEM((plane, made, model // plane), f32),
            pltpu.VMEM((plane, made, model // plane), f32),
            pltpu.VMEM((tokens, heads * vdim), bf16),
            dma((heads // group,)),
            dma((8,)),
            dma((n_ctx,)), dma((n_ctx,)),
            dma((n_ctx, n_role)), dma((n_ctx, n_role)),
            dma((n_ctx,)), dma((n_ctx,)),
            dma((n_ctx,)), dma((n_ctx,)),
            dma((plane,)), dma((plane,)),
        ],
        compiler_params=pltpu.CompilerParams(
            collective_id=0, has_side_effects=True, vmem_limit_bytes=56 * 1024 * 1024
        ),
    )(
        block_order, cache_length, block_dest,
        prompt_query.reshape(tokens * heads, width), prompt_latent, key_up, value_up, out_weight,
        step_query.reshape(made * heads, width), jnp.swapaxes(cache_latent, 1, 2), step_latent,
    )
    return pl.pallas_call(
        write_results,
        out_shape=(
            jax.ShapeDtypeStruct((tokens, heads * vdim), bf16),
            jax.ShapeDtypeStruct((steps, rows, model // plane), bf16),
        ),
        in_specs=[pl.BlockSpec(memory_space=pltpu.HBM), vmem],
        out_specs=(pl.BlockSpec(memory_space=pltpu.HBM), vmem),
        scratch_shapes=[dma(())],
        compiler_params=pltpu.CompilerParams(vmem_limit_bytes=56 * 1024 * 1024),
    )(prompt_made, step_made)


def solution(mesh):
    return jax.shard_map(
        per_device,
        mesh=mesh,
        in_specs=(
            P(("groups", "ctx"), ("head", "role"), None),
            P(("groups", "ctx"), None),
            P("groups"),
            P(("head", "role"), None, None),
            P(("head", "role"), None, None),
            P(("head", "role"), "ctx"),
            P(None, "groups", ("head", "role"), None),
            P("groups", "ctx", None),
            P(None, "groups", None),
            P("groups"),
            P("groups"),
        ),
        out_specs=(
            P(("groups", "ctx"), ("head", "role")),
            P(None, "groups", ("ctx", "head", "role")),
        ),
        check_vma=False,
    )
```

```python
import functools
import math

import jax
import jax.numpy as jnp
from jax import lax
from jax.experimental import pallas as pl
from jax.experimental.pallas import tpu as pltpu
from jax.sharding import PartitionSpec as P

MESH = pl.DeviceIdType.MESH
LOW = -1e30


def nt_dot(a, b):
    return lax.dot_general(a, b, (((1,), (1,)), ((), ())), preferred_element_type=jnp.float32)


def nn_dot(a, b):
    return jnp.dot(a, b, preferred_element_type=jnp.float32)


def quotient(x, n):
    return x >> (n.bit_length() - 1) if n & (n - 1) == 0 else lax.div(x, n)


def remainder(x, n):
    return x & (n - 1) if n & (n - 1) == 0 else lax.rem(x, n)


def one_hot_rows(count, source):
    out_row = lax.broadcasted_iota(jnp.int32, (count, count), 0)
    in_row = lax.broadcasted_iota(jnp.int32, (count, count), 1)
    return (in_row == source(out_row)).astype(jnp.bfloat16)


def kernel(
    size,
    order_ref, length_ref, dest_ref,
    pq_hbm, pl_hbm, ku_hbm, vu_hbm, ow_hbm, sq_hbm, cache_hbm, sl_ref,
    prompt_hbm, step_ref,
    pq, ku, vu, ow, sq, cache, own, keys, query, absorbed, step_rows, sums, stats, partials, flat, parts, landed,
    prompt, prompt_sem, local_sem, lat_send, lat_recv, fwd_send, fwd_recv, part_send, part_recv, stat_send, stat_recv, out_send, out_recv,
):
    n_ctx, n_head, n_role = size["ctx"], size["head"], size["role"]
    plane = n_head * n_role
    tokens, heads, nope, latent = size["tokens"], size["heads"], size["nope"], size["latent"]
    steps, rows, span, vdim = size["steps"], size["rows"], size["span"], size["vdim"]
    made = steps * rows
    half = tokens // n_role
    scale = (size["width"] ** -0.5) * math.log2(math.e)
    place, role = lax.axis_index("ctx"), lax.axis_index("role")
    here = lax.axis_index("head") * n_role + role

    def ctx_peer(k):
        return {"ctx": lax.rem(place + k, n_ctx)}

    def plane_peer(k):
        other = lax.rem(here + k, plane)
        return {"head": lax.div(other, n_role), "role": lax.rem(other, n_role)}

    started = iter(range(local_sem.shape[0]))

    def load(src, dst, pieces=1):
        copies = []
        step = src.shape[0] // pieces
        for i in range(pieces):
            part = pl.ds(i * step, step)
            copy = pltpu.make_async_copy(src.at[part], dst.at[part], local_sem.at[next(started)])
            copy.start()
            copies.append(copy)
        return copies

    (own_copy,) = load(pl_hbm, own)
    (sq_copy,) = load(sq_hbm, sq)
    pq_copies = load(pq_hbm, pq, 2)
    ku_copies = load(ku_hbm, ku, 4)
    cache_copies = load(cache_hbm, cache, rows)
    vu_copies = load(vu_hbm, vu, 4)
    ow_copies = load(ow_hbm, ow, 8)

    barrier = pltpu.get_barrier_semaphore()
    for k in range(1, n_ctx):
        pl.semaphore_signal(barrier, inc=1, device_id=ctx_peer(k), device_id_type=MESH)
    for k in range(1, plane):
        pl.semaphore_signal(barrier, inc=1, device_id=plane_peer(k), device_id_type=MESH)

    tile = 16

    def prompt_row(r):
        return remainder(r, tile) * heads + quotient(r, tile)

    def step_row(r):
        within = remainder(r, made)
        return (remainder(within, steps) * rows + quotient(within, steps)) * heads + quotient(r, made)

    sq_copy.wait()
    moved = nn_dot(one_hot_rows(made * heads, step_row), sq[...]).astype(jnp.bfloat16)
    query[:, tokens:, :] = moved.reshape(heads, made, size["width"])
    perm = one_hot_rows(tile * heads, prompt_row)
    for copy in pq_copies:
        copy.wait()
    for i in range(tokens // tile):
        moved = nn_dot(perm, pq[i * tile * heads : (i + 1) * tile * heads, :]).astype(jnp.bfloat16)
        query[:, i * tile : (i + 1) * tile, :] = moved.reshape(heads, tile, size["width"])

    pl.semaphore_wait(barrier, n_ctx - 1 + plane - 1)

    own_copy.wait()
    keys[pl.ds(pl.multiple_of(place * tokens, 16), tokens), :] = own[...]
    my_half = pl.multiple_of(role * half, 16)
    lat_copies = []
    for k in range(1, n_ctx):
        copy = pltpu.make_async_remote_copy(
            src_ref=own.at[pl.ds(my_half, half)],
            dst_ref=keys.at[pl.ds(pl.multiple_of(place * tokens + role * half, 16), half)],
            send_sem=lat_send.at[k], recv_sem=lat_recv.at[k],
            device_id=ctx_peer(k), device_id_type=MESH,
        )
        copy.start()
        lat_copies.append(copy)

    for h in range(heads):
        if h % (heads // 4) == 0:
            ku_copies[h // (heads // 4)].wait()
        low = nn_dot(query[h, :, :nope], ku[h]).astype(jnp.bfloat16)
        absorbed[h * tokens : (h + 1) * tokens, :latent] = low[:tokens]
        absorbed[h * tokens : (h + 1) * tokens, latent:] = query[h, :tokens, nope:]
        step_low = low[tokens:].astype(jnp.float32)
        step_high = query[h, tokens:, nope:].astype(jnp.float32)
        for b in range(rows):
            step_rows[b, h * steps : (h + 1) * steps, :latent] = step_low[b * steps : (b + 1) * steps]
            step_rows[b, h * steps : (h + 1) * steps, latent:] = step_high[b * steps : (b + 1) * steps]

    each = heads * steps
    count = rows * each
    row_id = lax.broadcasted_iota(jnp.int32, (count, 1), 0)
    row_step, row_request = remainder(row_id, steps), quotient(row_id, each)
    step_q = step_rows[...].astype(jnp.bfloat16)
    flat_q = step_q.reshape(count, step_q.shape[2])
    fresh = jnp.concatenate([sl_ref[u].astype(jnp.float32) for u in range(steps)], axis=0).astype(jnp.bfloat16)
    fresh_id = lax.broadcasted_iota(jnp.int32, (1, made), 1)
    fresh_mask = (remainder(fresh_id, rows) == row_request) & (quotient(fresh_id, rows) <= row_step) & (place == 0)
    fresh_scores = jnp.where(fresh_mask, nt_dot(flat_q, fresh) * scale, LOW)
    own_scores = jnp.where(row_request == dest_ref[place], nt_dot(flat_q, own[...]) * scale, LOW)
    for copy in cache_copies:
        copy.wait()
    cache_pos = place * span + lax.broadcasted_iota(jnp.int32, (1, span), 1)
    cache_scores = jnp.concatenate(
        [jnp.where(cache_pos < length_ref[b], nn_dot(step_q[b], cache[b]) * scale, LOW) for b in range(rows)], axis=0
    )
    peak = functools.reduce(
        jnp.maximum, [jnp.max(x, axis=1, keepdims=True) for x in (cache_scores, own_scores, fresh_scores)]
    )
    cache_w, own_w, fresh_w = (jnp.exp2(x - peak) for x in (cache_scores, own_scores, fresh_scores))
    amount = functools.reduce(jnp.add, [jnp.sum(x, axis=1, keepdims=True) for x in (cache_w, own_w, fresh_w)])
    cache_w = cache_w.astype(jnp.bfloat16)
    summed = nn_dot(own_w.astype(jnp.bfloat16), own[:, :latent]) + nn_dot(
        fresh_w.astype(jnp.bfloat16), fresh[:, :latent]
    )
    for b in range(rows):
        sums[b] = summed[b * each : (b + 1) * each] + nt_dot(
            cache_w[b * each : (b + 1) * each], cache[b, :latent, :]
        )
    lane = lax.broadcasted_iota(jnp.int32, (1, 128), 1)
    at_head = lane == quotient(remainder(row_id, each), steps)

    def by_head(column, other):
        spread = jnp.where(at_head, column, 0.0).reshape(rows, each // 8, 8, 128).sum(axis=1)
        table = jnp.concatenate(
            [
                functools.reduce(jnp.add, [spread[b, j : j + steps] for j in range(0, 8, steps)])
                for b in range(rows)
            ],
            axis=0,
        )
        return jnp.where(lane < heads, table, other)

    stats[0, :made] = by_head(peak, 0.0)
    stats[0, made:] = by_head(amount, 1.0)
    for h in range(heads):
        if h % (heads // 4) == 0:
            vu_copies[h // (heads // 4)].wait()
        mine = jnp.concatenate([sums[b, h * steps : (h + 1) * steps, :] for b in range(rows)], axis=0)
        partials[0, :, h * vdim : (h + 1) * vdim] = nn_dot(mine.astype(jnp.bfloat16), vu[h]).astype(jnp.bfloat16)
    part_copies = []
    for k in range(1, n_ctx):
        for src, send, recv in ((stats, stat_send, stat_recv), (partials, part_send, part_recv)):
            copy = pltpu.make_async_remote_copy(
                src_ref=src.at[0], dst_ref=src.at[k], send_sem=send.at[k], recv_sem=recv.at[k],
                device_id=ctx_peer(k), device_id_type=MESH,
            )
            copy.start()
            part_copies.append(copy)

    fwd_copies = []
    for k in range(1, n_ctx):
        lat_copies[k - 1].wait_recv()
        source = lax.rem(place + n_ctx - k, n_ctx)
        piece = keys.at[pl.ds(pl.multiple_of(source * tokens + role * half, 16), half)]
        for j in range(1, n_role):
            copy = pltpu.make_async_remote_copy(
                src_ref=piece, dst_ref=piece, send_sem=fwd_send.at[k, j], recv_sem=fwd_recv.at[k, j],
                device_id={"role": lax.rem(role + j, n_role)}, device_id_type=MESH,
            )
            copy.start()
            fwd_copies.append(copy)

    for copy in fwd_copies:
        copy.wait_recv()
    seq = n_ctx * tokens
    key_id = lax.broadcasted_iota(jnp.int32, (1, seq), 1)
    key_pos = jnp.zeros((1, seq), jnp.int32)
    for k in range(n_ctx):
        inside = (key_id >= k * tokens) & (key_id < (k + 1) * tokens)
        key_pos = jnp.where(inside, order_ref[k] * tokens + key_id - k * tokens, key_pos)
    query_pos = order_ref[place] * tokens + lax.broadcasted_iota(jnp.int32, (tokens, 1), 0)
    bias = jnp.where(key_pos <= query_pos, 0.0, LOW).astype(jnp.float32)
    group = size["group"]

    def prompt_scores(g):
        return nt_dot(absorbed[g * group * tokens : (g + 1) * group * tokens, :], keys[...])

    prompt_copies = []

    def prompt_finish(g, s):
        s = (s * scale).reshape(group, tokens, seq) + bias[None]
        w = jnp.exp2(s - jnp.max(s, axis=2, keepdims=True))
        inverse = 1.0 / jnp.sum(w, axis=2, keepdims=True)
        o = nn_dot(w.astype(jnp.bfloat16).reshape(group * tokens, seq), keys[:, :latent])
        attended = (o.reshape(group, tokens, latent) * inverse).astype(jnp.bfloat16)
        for i in range(group):
            h = g * group + i
            prompt[:, h * vdim : (h + 1) * vdim] = nn_dot(attended[i], vu[h]).astype(jnp.bfloat16)
        cols = slice(g * group * vdim, (g + 1) * group * vdim)
        copy = pltpu.make_async_copy(prompt.at[:, cols], prompt_hbm.at[:, cols], prompt_sem.at[g])
        copy.start()
        prompt_copies.append(copy)

    n_groups = heads // group
    first = n_groups // 2
    ahead = prompt_scores(0)
    for g in range(first):
        current, ahead = ahead, prompt_scores(g + 1)
        prompt_finish(g, current)

    for copy in part_copies:
        copy.wait_recv()
    top = stats[0, :made]
    for k in range(1, n_ctx):
        top = jnp.maximum(top, stats[k, :made])
    factors = [jnp.exp2(stats[k, :made] - top) for k in range(n_ctx)]
    whole = functools.reduce(jnp.add, [factors[k] * stats[k, made:] for k in range(n_ctx)])
    factors = [f / whole for f in factors]
    for h in range(heads):
        cols = slice(h * vdim, (h + 1) * vdim)
        merged = functools.reduce(
            jnp.add, [partials[k, :, cols].astype(jnp.float32) * factors[k][:, h : h + 1] for k in range(n_ctx)]
        )
        flat[:, cols] = merged.astype(jnp.bfloat16)
    for copy in ow_copies:
        copy.wait()
    in_order = one_hot_rows(made, lambda r: remainder(r, rows) * steps + quotient(r, rows))
    projected = nn_dot(nn_dot(in_order, flat[...]).astype(jnp.bfloat16), ow[...])
    width = projected.shape[1] // plane
    for d in range(plane):
        parts[d] = projected[:, d * width : (d + 1) * width]
    out_copies = []
    for k in range(1, plane):
        copy = pltpu.make_async_remote_copy(
            src_ref=parts.at[lax.rem(here + k, plane)], dst_ref=landed.at[k],
            send_sem=out_send.at[k], recv_sem=out_recv.at[k],
            device_id=plane_peer(k), device_id_type=MESH,
        )
        copy.start()
        out_copies.append(copy)

    for g in range(first, n_groups):
        current, ahead = ahead, prompt_scores(g + 1) if g + 1 < n_groups else None
        prompt_finish(g, current)

    result = parts[here]
    for k in range(1, plane):
        out_copies[k - 1].wait_recv()
        result = result + landed[k]
    step_ref[...] = result
    for copy in lat_copies + fwd_copies + part_copies + out_copies:
        copy.wait_send()
    for copy in prompt_copies:
        copy.wait()


def write_results(prompt_in, step_in, prompt_out, step_out):
    prompt_out[...] = prompt_in[...]
    steps, rows = step_out.shape[:2]
    for t in range(steps):
        step_out[t] = step_in[t * rows : (t + 1) * rows, :].astype(step_out.dtype)


def per_device(
    prompt_query, prompt_latent, block_order, key_up, value_up, out_weight,
    step_query, cache_latent, step_latent, cache_length, block_dest,
):
    tokens, heads, width = prompt_query.shape
    nope, latent = key_up.shape[1:]
    vdim = value_up.shape[2]
    steps, rows = step_query.shape[:2]
    span, key_width = cache_latent.shape[1:]
    model = out_weight.shape[1]
    n_ctx, n_head, n_role = (lax.axis_size(a) for a in ("ctx", "head", "role"))
    plane, made, seq = n_head * n_role, steps * rows, n_ctx * tokens
    group = 4 if heads % 4 == 0 and seq <= 512 else 1
    size = dict(
        ctx=n_ctx, head=n_head, role=n_role, tokens=tokens, heads=heads, width=width, nope=nope,
        latent=latent, vdim=vdim, steps=steps, rows=rows, span=span, group=group,
    )
    bf16, f32 = jnp.bfloat16, jnp.float32
    smem, anywhere, vmem = (pl.BlockSpec(memory_space=m) for m in (pltpu.SMEM, pl.ANY, pltpu.VMEM))
    dma = pltpu.SemaphoreType.DMA
    prompt_made, step_made = pl.pallas_call(
        functools.partial(kernel, size),
        out_shape=(
            jax.ShapeDtypeStruct((tokens, heads * vdim), bf16),
            jax.ShapeDtypeStruct((made, model // plane), f32),
        ),
        in_specs=[smem] * 3 + [anywhere] * 7 + [vmem],
        out_specs=(anywhere, vmem),
        scratch_shapes=[
            pltpu.VMEM((tokens * heads, width), bf16),
            pltpu.VMEM(key_up.shape, bf16),
            pltpu.VMEM(value_up.shape, bf16),
            pltpu.VMEM(out_weight.shape, bf16),
            pltpu.VMEM((made * heads, width), bf16),
            pltpu.VMEM((rows, key_width, span), bf16),
            pltpu.VMEM((tokens, key_width), bf16),
            pltpu.VMEM((seq, key_width), bf16),
            pltpu.VMEM((heads, tokens + made, width), bf16),
            pltpu.VMEM((heads * tokens, key_width), bf16),
            pltpu.VMEM((rows, heads * steps, key_width), f32),
            pltpu.VMEM((rows, heads * steps, latent), f32),
            pltpu.VMEM((n_ctx, 2 * made, 128), f32),
            pltpu.VMEM((n_ctx, made, heads * vdim), bf16),
            pltpu.VMEM((made, heads * vdim), bf16),
            pltpu.VMEM((plane, made, model // plane), f32),
            pltpu.VMEM((plane, made, model // plane), f32),
            pltpu.VMEM((tokens, heads * vdim), bf16),
            dma((heads // group,)),
            dma((20 + rows,)),
            dma((n_ctx,)), dma((n_ctx,)),
            dma((n_ctx, n_role)), dma((n_ctx, n_role)),
            dma((n_ctx,)), dma((n_ctx,)),
            dma((n_ctx,)), dma((n_ctx,)),
            dma((plane,)), dma((plane,)),
        ],
        compiler_params=pltpu.CompilerParams(
            collective_id=0, has_side_effects=True, vmem_limit_bytes=56 * 1024 * 1024
        ),
    )(
        block_order, cache_length, block_dest,
        prompt_query.reshape(tokens * heads, width), prompt_latent, key_up, value_up, out_weight,
        step_query.reshape(made * heads, width), jnp.swapaxes(cache_latent, 1, 2), step_latent,
    )
    return pl.pallas_call(
        write_results,
        out_shape=(
            jax.ShapeDtypeStruct((tokens, heads * vdim), bf16),
            jax.ShapeDtypeStruct((steps, rows, model // plane), bf16),
        ),
        in_specs=[vmem, vmem],
        out_specs=(vmem, vmem),
        compiler_params=pltpu.CompilerParams(vmem_limit_bytes=56 * 1024 * 1024),
    )(prompt_made, step_made)


def solution(mesh):
    return jax.shard_map(
        per_device,
        mesh=mesh,
        in_specs=(
            P(("groups", "ctx"), ("head", "role"), None),
            P(("groups", "ctx"), None),
            P("groups"),
            P(("head", "role"), None, None),
            P(("head", "role"), None, None),
            P(("head", "role"), "ctx"),
            P(None, "groups", ("head", "role"), None),
            P("groups", "ctx", None),
            P(None, "groups", None),
            P("groups"),
            P("groups"),
        ),
        out_specs=(
            P(("groups", "ctx"), ("head", "role")),
            P(None, "groups", ("ctx", "head", "role")),
        ),
        check_vma=False,
    )
```

```python
import functools
import math

import jax
import jax.numpy as jnp
from jax import lax
from jax.experimental import pallas as pl
from jax.experimental.pallas import tpu as pltpu
from jax.sharding import PartitionSpec as P

MESH = pl.DeviceIdType.MESH
LOW = -1e30


def nt_dot(a, b):
    return lax.dot_general(a, b, (((1,), (1,)), ((), ())), preferred_element_type=jnp.float32)


def nn_dot(a, b):
    return jnp.dot(a, b, preferred_element_type=jnp.float32)


def quotient(x, n):
    return x >> (n.bit_length() - 1) if n & (n - 1) == 0 else lax.div(x, n)


def remainder(x, n):
    return x & (n - 1) if n & (n - 1) == 0 else lax.rem(x, n)


def one_hot_rows(count, source):
    out_row = lax.broadcasted_iota(jnp.int32, (count, count), 0)
    in_row = lax.broadcasted_iota(jnp.int32, (count, count), 1)
    return (in_row == source(out_row)).astype(jnp.bfloat16)


def kernel(
    size,
    order_ref, length_ref, dest_ref,
    pq_hbm, pl_hbm, ku_hbm, vu_hbm, ow_hbm, sq_hbm, cache_hbm, sl_ref,
    prompt_hbm, step_ref,
    pq, ku, vu, ow, sq, cache, own, keys, query, absorbed, step_rows, sums, stats, part_out, part_in, flat, parts, landed,
    prompt, prompt_sem, local_sem, lat_send, lat_recv, fwd_send, fwd_recv, part_send, part_recv, stat_send, stat_recv, flat_send, flat_recv, out_send, out_recv,
):
    n_ctx, n_head, n_role = size["ctx"], size["head"], size["role"]
    plane = n_head * n_role
    tokens, heads, nope, latent = size["tokens"], size["heads"], size["nope"], size["latent"]
    steps, rows, span, vdim = size["steps"], size["rows"], size["span"], size["vdim"]
    made = steps * rows
    half = tokens // n_role
    scale = (size["width"] ** -0.5) * math.log2(math.e)
    place, role = lax.axis_index("ctx"), lax.axis_index("role")
    here = lax.axis_index("head") * n_role + role
    shares = size["shares"]
    per = heads // shares
    mine_at = place if shares > 1 else 0

    def ctx_peer(k):
        return {"ctx": lax.rem(place + k, n_ctx)}

    def plane_peer(k):
        other = lax.rem(here + k, plane)
        return {"head": lax.div(other, n_role), "role": lax.rem(other, n_role)}

    started = iter(range(local_sem.shape[0]))

    def load(src, dst, pieces=1):
        copies = []
        step = src.shape[0] // pieces
        for i in range(pieces):
            part = pl.ds(i * step, step)
            copy = pltpu.make_async_copy(src.at[part], dst.at[part], local_sem.at[next(started)])
            copy.start()
            copies.append(copy)
        return copies

    (own_copy,) = load(pl_hbm, own)
    (sq_copy,) = load(sq_hbm, sq)
    pq_copies = load(pq_hbm, pq, 2)
    ku_copies = load(ku_hbm, ku, 4)
    cache_copies = load(cache_hbm, cache, rows)
    vu_copies = load(vu_hbm, vu, 4)
    ow_copies = load(ow_hbm, ow, 8)

    barrier = pltpu.get_barrier_semaphore()
    for k in range(1, n_ctx):
        pl.semaphore_signal(barrier, inc=1, device_id=ctx_peer(k), device_id_type=MESH)
    for k in range(1, plane):
        pl.semaphore_signal(barrier, inc=1, device_id=plane_peer(k), device_id_type=MESH)

    pl.semaphore_wait(barrier, n_ctx - 1 + plane - 1)

    own_copy.wait()
    keys[pl.ds(pl.multiple_of(place * tokens, 16), tokens), :] = own[...]
    my_half = pl.multiple_of(role * half, 16)
    lat_copies = []
    for k in range(1, n_ctx):
        copy = pltpu.make_async_remote_copy(
            src_ref=own.at[pl.ds(my_half, half)],
            dst_ref=keys.at[pl.ds(pl.multiple_of(place * tokens + role * half, 16), half)],
            send_sem=lat_send.at[k], recv_sem=lat_recv.at[k],
            device_id=ctx_peer(k), device_id_type=MESH,
        )
        copy.start()
        lat_copies.append(copy)

    tile = 16

    def prompt_row(r):
        return remainder(r, tile) * heads + quotient(r, tile)

    def step_row(r):
        within = remainder(r, made)
        return (remainder(within, steps) * rows + quotient(within, steps)) * heads + quotient(r, made)

    sq_copy.wait()
    moved = nn_dot(one_hot_rows(made * heads, step_row), sq[...]).astype(jnp.bfloat16)
    query[:, tokens:, :] = moved.reshape(heads, made, size["width"])
    perm = one_hot_rows(tile * heads, prompt_row)
    for copy in pq_copies:
        copy.wait()
    for i in range(tokens // tile):
        moved = nn_dot(perm, pq[i * tile * heads : (i + 1) * tile * heads, :]).astype(jnp.bfloat16)
        query[:, i * tile : (i + 1) * tile, :] = moved.reshape(heads, tile, size["width"])

    for h in range(heads):
        if h % (heads // 4) == 0:
            ku_copies[h // (heads // 4)].wait()
        low = nn_dot(query[h, :, :nope], ku[h]).astype(jnp.bfloat16)
        absorbed[h * tokens : (h + 1) * tokens, :latent] = low[:tokens]
        absorbed[h * tokens : (h + 1) * tokens, latent:] = query[h, :tokens, nope:]
        step_low = low[tokens:].astype(jnp.float32)
        step_high = query[h, tokens:, nope:].astype(jnp.float32)
        for b in range(rows):
            step_rows[b, h * steps : (h + 1) * steps, :latent] = step_low[b * steps : (b + 1) * steps]
            step_rows[b, h * steps : (h + 1) * steps, latent:] = step_high[b * steps : (b + 1) * steps]

    each = heads * steps
    count = rows * each
    row_id = lax.broadcasted_iota(jnp.int32, (count, 1), 0)
    row_step, row_request = remainder(row_id, steps), quotient(row_id, each)
    step_q = step_rows[...].astype(jnp.bfloat16)
    flat_q = step_q.reshape(count, step_q.shape[2])
    fresh = jnp.concatenate([sl_ref[u].astype(jnp.float32) for u in range(steps)], axis=0).astype(jnp.bfloat16)
    fresh_id = lax.broadcasted_iota(jnp.int32, (1, made), 1)
    fresh_mask = (remainder(fresh_id, rows) == row_request) & (quotient(fresh_id, rows) <= row_step) & (place == 0)
    fresh_scores = jnp.where(fresh_mask, nt_dot(flat_q, fresh) * scale, LOW)
    own_scores = jnp.where(row_request == dest_ref[place], nt_dot(flat_q, own[...]) * scale, LOW)
    for copy in cache_copies:
        copy.wait()
    cache_pos = place * span + lax.broadcasted_iota(jnp.int32, (1, span), 1)
    cache_scores = jnp.concatenate(
        [jnp.where(cache_pos < length_ref[b], nn_dot(step_q[b], cache[b]) * scale, LOW) for b in range(rows)], axis=0
    )
    peak = functools.reduce(
        jnp.maximum, [jnp.max(x, axis=1, keepdims=True) for x in (cache_scores, own_scores, fresh_scores)]
    )
    cache_w, own_w, fresh_w = (jnp.exp2(x - peak) for x in (cache_scores, own_scores, fresh_scores))
    amount = functools.reduce(jnp.add, [jnp.sum(x, axis=1, keepdims=True) for x in (cache_w, own_w, fresh_w)])
    cache_w = cache_w.astype(jnp.bfloat16)
    summed = nn_dot(own_w.astype(jnp.bfloat16), own[:, :latent]) + nn_dot(
        fresh_w.astype(jnp.bfloat16), fresh[:, :latent]
    )
    for b in range(rows):
        sums[b] = summed[b * each : (b + 1) * each] + nt_dot(
            cache_w[b * each : (b + 1) * each], cache[b, :latent, :]
        )
    lane = lax.broadcasted_iota(jnp.int32, (1, 128), 1)
    row_head = quotient(remainder(row_id, each), steps)
    spread = jnp.where(lane == row_head, peak, jnp.where(lane == 64 + row_head, amount, 0.0))
    spread = spread.reshape(rows, each // 8, 8, 128).sum(axis=1)
    stats[0] = jnp.concatenate(
        [functools.reduce(jnp.add, [spread[b, j : j + steps] for j in range(0, 8, steps)]) for b in range(rows)],
        axis=0,
    )
    for h in range(heads):
        if h % (heads // 4) == 0:
            vu_copies[h // (heads // 4)].wait()
        mine = jnp.concatenate([sums[b, h * steps : (h + 1) * steps, :] for b in range(rows)], axis=0)
        at = (h % per) * vdim
        part_out[h // per, :, at : at + vdim] = nn_dot(mine.astype(jnp.bfloat16), vu[h]).astype(jnp.bfloat16)
    part_copies, flat_copies = [], []
    for k in range(1, n_ctx):
        target = lax.rem(place + k, n_ctx) if shares > 1 else 0
        for src, dst, send, recv in (
            (stats.at[0], stats.at[k], stat_send, stat_recv),
            (part_out.at[target], part_in.at[k], part_send, part_recv),
        ):
            copy = pltpu.make_async_remote_copy(
                src_ref=src, dst_ref=dst, send_sem=send.at[k], recv_sem=recv.at[k],
                device_id=ctx_peer(k), device_id_type=MESH,
            )
            copy.start()
            part_copies.append(copy)

    fwd_copies = []
    for k in range(1, n_ctx):
        lat_copies[k - 1].wait_recv()
        source = lax.rem(place + n_ctx - k, n_ctx)
        piece = keys.at[pl.ds(pl.multiple_of(source * tokens + role * half, 16), half)]
        for j in range(1, n_role):
            copy = pltpu.make_async_remote_copy(
                src_ref=piece, dst_ref=piece, send_sem=fwd_send.at[k, j], recv_sem=fwd_recv.at[k, j],
                device_id={"role": lax.rem(role + j, n_role)}, device_id_type=MESH,
            )
            copy.start()
            fwd_copies.append(copy)

    for copy in fwd_copies:
        copy.wait_recv()
    seq = n_ctx * tokens
    key_id = lax.broadcasted_iota(jnp.int32, (1, seq), 1)
    key_pos = jnp.zeros((1, seq), jnp.int32)
    for k in range(n_ctx):
        inside = (key_id >= k * tokens) & (key_id < (k + 1) * tokens)
        key_pos = jnp.where(inside, order_ref[k] * tokens + key_id - k * tokens, key_pos)
    query_pos = order_ref[place] * tokens + lax.broadcasted_iota(jnp.int32, (tokens, 1), 0)
    bias = jnp.where(key_pos <= query_pos, 0.0, LOW).astype(jnp.float32)
    group = size["group"]

    def prompt_scores(g):
        return nt_dot(absorbed[g * group * tokens : (g + 1) * group * tokens, :], keys[...])

    prompt_copies = []

    def prompt_finish(g, s):
        s = (s * scale).reshape(group, tokens, seq) + bias[None]
        w = jnp.exp2(s - jnp.max(s, axis=2, keepdims=True))
        inverse = 1.0 / jnp.sum(w, axis=2, keepdims=True)
        o = nn_dot(w.astype(jnp.bfloat16).reshape(group * tokens, seq), keys[:, :latent])
        attended = (o.reshape(group, tokens, latent) * inverse).astype(jnp.bfloat16)
        for i in range(group):
            h = g * group + i
            prompt[:, h * vdim : (h + 1) * vdim] = nn_dot(attended[i], vu[h]).astype(jnp.bfloat16)
        cols = slice(g * group * vdim, (g + 1) * group * vdim)
        copy = pltpu.make_async_copy(prompt.at[:, cols], prompt_hbm.at[:, cols], prompt_sem.at[g])
        copy.start()
        prompt_copies.append(copy)

    def merge():
        for copy in part_copies:
            copy.wait_recv()
        peaks = [stats[k, :, :heads] for k in range(n_ctx)]
        top = functools.reduce(jnp.maximum, peaks)
        factors = [jnp.exp2(p - top) for p in peaks]
        whole = functools.reduce(jnp.add, [factors[k] * stats[k, :, 64 : 64 + heads] for k in range(n_ctx)])
        factors = [f / whole for f in factors]
        head_lane = lax.broadcasted_iota(jnp.int32, (made, heads), 1)
        pieces = []
        for j in range(per):
            wanted = head_lane == (place * per + j if shares > 1 else j)
            merged = jnp.zeros((made, vdim), jnp.float32)
            for k in range(n_ctx):
                factor = jnp.sum(jnp.where(wanted, factors[k], 0.0), axis=1, keepdims=True)
                cols = slice(j * vdim, (j + 1) * vdim)
                part = part_in[k, :, cols] if k else part_out[mine_at, :, cols]
                merged = merged + part.astype(jnp.float32) * factor
            pieces.append(merged.astype(jnp.bfloat16))
        in_order = one_hot_rows(made, lambda r: remainder(r, rows) * steps + quotient(r, rows))
        flat[mine_at] = nn_dot(in_order, jnp.concatenate(pieces, axis=1)).astype(jnp.bfloat16)
        for k in range(1, n_ctx if shares > 1 else 1):
            copy = pltpu.make_async_remote_copy(
                src_ref=flat.at[mine_at], dst_ref=flat.at[mine_at], send_sem=flat_send.at[k], recv_sem=flat_recv.at[k],
                device_id=ctx_peer(k), device_id_type=MESH,
            )
            copy.start()
            flat_copies.append(copy)

    n_groups = heads // group
    first = max(n_groups // 2, 1)
    ahead = prompt_scores(0)
    for g in range(first):
        current, ahead = ahead, prompt_scores(g + 1) if g + 1 < n_groups else None
        prompt_finish(g, current)
        if g == 0:
            merge()

    for copy in flat_copies:
        copy.wait_recv()
    for copy in ow_copies:
        copy.wait()
    projected = nn_dot(jnp.concatenate([flat[c] for c in range(shares)], axis=1), ow[...])
    width = projected.shape[1] // plane
    for d in range(plane):
        parts[d] = projected[:, d * width : (d + 1) * width]
    out_copies = []
    for k in range(1, plane):
        copy = pltpu.make_async_remote_copy(
            src_ref=parts.at[lax.rem(here + k, plane)], dst_ref=landed.at[k],
            send_sem=out_send.at[k], recv_sem=out_recv.at[k],
            device_id=plane_peer(k), device_id_type=MESH,
        )
        copy.start()
        out_copies.append(copy)

    for g in range(first, n_groups):
        current, ahead = ahead, prompt_scores(g + 1) if g + 1 < n_groups else None
        prompt_finish(g, current)

    result = parts[here]
    for k in range(1, plane):
        out_copies[k - 1].wait_recv()
        result = result + landed[k]
    step_ref[...] = result
    for copy in lat_copies + fwd_copies + part_copies + flat_copies + out_copies:
        copy.wait_send()
    for copy in prompt_copies:
        copy.wait()


def write_results(prompt_in, step_in, prompt_out, step_out):
    prompt_out[...] = prompt_in[...]
    steps, rows = step_out.shape[:2]
    for t in range(steps):
        step_out[t] = step_in[t * rows : (t + 1) * rows, :].astype(step_out.dtype)


def per_device(
    prompt_query, prompt_latent, block_order, key_up, value_up, out_weight,
    step_query, cache_latent, step_latent, cache_length, block_dest,
):
    tokens, heads, width = prompt_query.shape
    nope, latent = key_up.shape[1:]
    vdim = value_up.shape[2]
    steps, rows = step_query.shape[:2]
    span, key_width = cache_latent.shape[1:]
    model = out_weight.shape[1]
    n_ctx, n_head, n_role = (lax.axis_size(a) for a in ("ctx", "head", "role"))
    plane, made, seq = n_head * n_role, steps * rows, n_ctx * tokens
    shares = n_ctx if heads % n_ctx == 0 else 1
    group = 4 if heads % 4 == 0 and seq <= 512 else 1
    size = dict(
        ctx=n_ctx, head=n_head, role=n_role, tokens=tokens, heads=heads, width=width, nope=nope,
        latent=latent, vdim=vdim, steps=steps, rows=rows, span=span, group=group, shares=shares,
    )
    bf16, f32 = jnp.bfloat16, jnp.float32
    smem, anywhere, vmem = (pl.BlockSpec(memory_space=m) for m in (pltpu.SMEM, pl.ANY, pltpu.VMEM))
    dma = pltpu.SemaphoreType.DMA
    prompt_made, step_made = pl.pallas_call(
        functools.partial(kernel, size),
        out_shape=(
            jax.ShapeDtypeStruct((tokens, heads * vdim), bf16),
            jax.ShapeDtypeStruct((made, model // plane), f32),
        ),
        in_specs=[smem] * 3 + [anywhere] * 7 + [vmem],
        out_specs=(anywhere, vmem),
        scratch_shapes=[
            pltpu.VMEM((tokens * heads, width), bf16),
            pltpu.VMEM(key_up.shape, bf16),
            pltpu.VMEM(value_up.shape, bf16),
            pltpu.VMEM(out_weight.shape, bf16),
            pltpu.VMEM((made * heads, width), bf16),
            pltpu.VMEM((rows, key_width, span), bf16),
            pltpu.VMEM((tokens, key_width), bf16),
            pltpu.VMEM((seq, key_width), bf16),
            pltpu.VMEM((heads, tokens + made, width), bf16),
            pltpu.VMEM((heads * tokens, key_width), bf16),
            pltpu.VMEM((rows, heads * steps, key_width), f32),
            pltpu.VMEM((rows, heads * steps, latent), f32),
            pltpu.VMEM((n_ctx, made, 128), f32),
            pltpu.VMEM((shares, made, heads * vdim // shares), bf16),
            pltpu.VMEM((n_ctx, made, heads * vdim // shares), bf16),
            pltpu.VMEM((shares, made, heads * vdim // shares), bf16),
            pltpu.VMEM((plane, made, model // plane), f32),
            pltpu.VMEM((plane, made, model // plane), f32),
            pltpu.VMEM((tokens, heads * vdim), bf16),
            dma((heads // group,)),
            dma((20 + rows,)),
            dma((n_ctx,)), dma((n_ctx,)),
            dma((n_ctx, n_role)), dma((n_ctx, n_role)),
            dma((n_ctx,)), dma((n_ctx,)),
            dma((n_ctx,)), dma((n_ctx,)),
            dma((n_ctx,)), dma((n_ctx,)),
            dma((plane,)), dma((plane,)),
        ],
        compiler_params=pltpu.CompilerParams(
            collective_id=0, has_side_effects=True, vmem_limit_bytes=56 * 1024 * 1024
        ),
    )(
        block_order, cache_length, block_dest,
        prompt_query.reshape(tokens * heads, width), prompt_latent, key_up, value_up, out_weight,
        step_query.reshape(made * heads, width), jnp.swapaxes(cache_latent, 1, 2), step_latent,
    )
    return pl.pallas_call(
        write_results,
        out_shape=(
            jax.ShapeDtypeStruct((tokens, heads * vdim), bf16),
            jax.ShapeDtypeStruct((steps, rows, model // plane), bf16),
        ),
        in_specs=[vmem, vmem],
        out_specs=(vmem, vmem),
        compiler_params=pltpu.CompilerParams(vmem_limit_bytes=56 * 1024 * 1024),
    )(prompt_made, step_made)


def solution(mesh):
    return jax.shard_map(
        per_device,
        mesh=mesh,
        in_specs=(
            P(("groups", "ctx"), ("head", "role"), None),
            P(("groups", "ctx"), None),
            P("groups"),
            P(("head", "role"), None, None),
            P(("head", "role"), None, None),
            P(("head", "role"), "ctx"),
            P(None, "groups", ("head", "role"), None),
            P("groups", "ctx", None),
            P(None, "groups", None),
            P("groups"),
            P("groups"),
        ),
        out_specs=(
            P(("groups", "ctx"), ("head", "role")),
            P(None, "groups", ("ctx", "head", "role")),
        ),
        check_vma=False,
    )
```

```python
import functools
import math

import jax
import jax.numpy as jnp
from jax import lax
from jax.experimental import pallas as pl
from jax.experimental.pallas import tpu as pltpu
from jax.sharding import PartitionSpec as P

MESH = pl.DeviceIdType.MESH
LOW = -1e30


def nt_dot(a, b):
    return lax.dot_general(a, b, (((1,), (1,)), ((), ())), preferred_element_type=jnp.float32)


def nn_dot(a, b):
    return jnp.dot(a, b, preferred_element_type=jnp.float32)


def quotient(x, n):
    return x >> (n.bit_length() - 1) if n & (n - 1) == 0 else lax.div(x, n)


def remainder(x, n):
    return x & (n - 1) if n & (n - 1) == 0 else lax.rem(x, n)


def one_hot_rows(count, source):
    out_row = lax.broadcasted_iota(jnp.int32, (count, count), 0)
    in_row = lax.broadcasted_iota(jnp.int32, (count, count), 1)
    return (in_row == source(out_row)).astype(jnp.bfloat16)


def kernel(
    size,
    order_ref, length_ref, dest_ref,
    pq_hbm, pl_hbm, ku_hbm, vu_hbm, ow_hbm, sq_hbm, cache_hbm, sl_ref,
    prompt_hbm, step_ref,
    pq, ku, vu, ow, sq, cache, own, keys, query, absorbed, step_rows, sums, stats, part_out, part_in, flat, parts, landed,
    prompt, keys_t, prompt_sem, local_sem, lat_send, lat_recv, fwd_send, fwd_recv, part_send, part_recv, stat_send, stat_recv, flat_send, flat_recv, out_send, out_recv,
):
    n_ctx, n_head, n_role = size["ctx"], size["head"], size["role"]
    plane = n_head * n_role
    tokens, heads, nope, latent = size["tokens"], size["heads"], size["nope"], size["latent"]
    steps, rows, span, vdim = size["steps"], size["rows"], size["span"], size["vdim"]
    made = steps * rows
    half = tokens // n_role
    scale = (size["width"] ** -0.5) * math.log2(math.e)
    place, role = lax.axis_index("ctx"), lax.axis_index("role")
    here = lax.axis_index("head") * n_role + role
    shares = size["shares"]
    per = heads // shares
    mine_at = place if shares > 1 else 0

    def ctx_peer(k):
        return {"ctx": lax.rem(place + k, n_ctx)}

    def plane_peer(k):
        other = lax.rem(here + k, plane)
        return {"head": lax.div(other, n_role), "role": lax.rem(other, n_role)}

    started = iter(range(local_sem.shape[0]))

    def load(src, dst, pieces=1):
        copies = []
        step = src.shape[0] // pieces
        for i in range(pieces):
            part = pl.ds(i * step, step)
            copy = pltpu.make_async_copy(src.at[part], dst.at[part], local_sem.at[next(started)])
            copy.start()
            copies.append(copy)
        return copies

    (own_copy,) = load(pl_hbm, own)
    (sq_copy,) = load(sq_hbm, sq)
    pq_copies = load(pq_hbm, pq, 2)
    ku_copies = load(ku_hbm, ku, 4)
    cache_copies = load(cache_hbm, cache, rows)
    vu_copies = load(vu_hbm, vu, 4)
    ow_copies = load(ow_hbm, ow, 8)

    barrier = pltpu.get_barrier_semaphore()
    for k in range(1, n_ctx):
        pl.semaphore_signal(barrier, inc=1, device_id=ctx_peer(k), device_id_type=MESH)
    for k in range(1, plane):
        pl.semaphore_signal(barrier, inc=1, device_id=plane_peer(k), device_id_type=MESH)

    pl.semaphore_wait(barrier, n_ctx - 1 + plane - 1)

    own_copy.wait()
    keys[pl.ds(pl.multiple_of(place * tokens, 16), tokens), :] = own[...]
    my_half = pl.multiple_of(role * half, 16)
    lat_copies = []
    for k in range(1, n_ctx):
        copy = pltpu.make_async_remote_copy(
            src_ref=own.at[pl.ds(my_half, half)],
            dst_ref=keys.at[pl.ds(pl.multiple_of(place * tokens + role * half, 16), half)],
            send_sem=lat_send.at[k], recv_sem=lat_recv.at[k],
            device_id=ctx_peer(k), device_id_type=MESH,
        )
        copy.start()
        lat_copies.append(copy)

    tile = 16

    def prompt_row(r):
        return remainder(r, tile) * heads + quotient(r, tile)

    def step_row(r):
        within = remainder(r, made)
        return (remainder(within, steps) * rows + quotient(within, steps)) * heads + quotient(r, made)

    sq_copy.wait()
    moved = nn_dot(one_hot_rows(made * heads, step_row), sq[...]).astype(jnp.bfloat16)
    query[:, tokens:, :] = moved.reshape(heads, made, size["width"])
    perm = one_hot_rows(tile * heads, prompt_row)
    for copy in pq_copies:
        copy.wait()
    for i in range(tokens // tile):
        moved = nn_dot(perm, pq[i * tile * heads : (i + 1) * tile * heads, :]).astype(jnp.bfloat16)
        query[:, i * tile : (i + 1) * tile, :] = moved.reshape(heads, tile, size["width"])

    for h in range(heads):
        if h % (heads // 4) == 0:
            ku_copies[h // (heads // 4)].wait()
        low = nn_dot(query[h, :, :nope], ku[h]).astype(jnp.bfloat16)
        absorbed[h * tokens : (h + 1) * tokens, :latent] = low[:tokens]
        absorbed[h * tokens : (h + 1) * tokens, latent:] = query[h, :tokens, nope:]
        step_low = low[tokens:].astype(jnp.float32)
        step_high = query[h, tokens:, nope:].astype(jnp.float32)
        for b in range(rows):
            step_rows[b, h * steps : (h + 1) * steps, :latent] = step_low[b * steps : (b + 1) * steps]
            step_rows[b, h * steps : (h + 1) * steps, latent:] = step_high[b * steps : (b + 1) * steps]

    each = heads * steps
    count = rows * each
    row_id = lax.broadcasted_iota(jnp.int32, (count, 1), 0)
    row_step, row_request = remainder(row_id, steps), quotient(row_id, each)
    step_q = step_rows[...].astype(jnp.bfloat16)
    flat_q = step_q.reshape(count, step_q.shape[2])
    fresh = jnp.concatenate([sl_ref[u].astype(jnp.float32) for u in range(steps)], axis=0).astype(jnp.bfloat16)
    fresh_id = lax.broadcasted_iota(jnp.int32, (1, made), 1)
    fresh_mask = (remainder(fresh_id, rows) == row_request) & (quotient(fresh_id, rows) <= row_step) & (place == 0)
    fresh_scores = jnp.where(fresh_mask, nt_dot(flat_q, fresh) * scale, LOW)
    own_scores = jnp.where(row_request == dest_ref[place], nt_dot(flat_q, own[...]) * scale, LOW)
    for copy in cache_copies:
        copy.wait()
    cache_pos = place * span + lax.broadcasted_iota(jnp.int32, (1, span), 1)
    cache_scores = jnp.concatenate(
        [jnp.where(cache_pos < length_ref[b], nn_dot(step_q[b], cache[b]) * scale, LOW) for b in range(rows)], axis=0
    )
    peak = functools.reduce(
        jnp.maximum, [jnp.max(x, axis=1, keepdims=True) for x in (cache_scores, own_scores, fresh_scores)]
    )
    cache_w, own_w, fresh_w = (jnp.exp2(x - peak) for x in (cache_scores, own_scores, fresh_scores))
    amount = functools.reduce(jnp.add, [jnp.sum(x, axis=1, keepdims=True) for x in (cache_w, own_w, fresh_w)])
    cache_w = cache_w.astype(jnp.bfloat16)
    summed = nn_dot(own_w.astype(jnp.bfloat16), own[:, :latent]) + nn_dot(
        fresh_w.astype(jnp.bfloat16), fresh[:, :latent]
    )
    for b in range(rows):
        sums[b] = summed[b * each : (b + 1) * each] + nt_dot(
            cache_w[b * each : (b + 1) * each], cache[b, :latent, :]
        )
    lane = lax.broadcasted_iota(jnp.int32, (1, 128), 1)
    row_head = quotient(remainder(row_id, each), steps)
    spread = jnp.where(lane == row_head, peak, jnp.where(lane == 64 + row_head, amount, 0.0))
    spread = spread.reshape(rows, each // 8, 8, 128).sum(axis=1)
    stats[0] = jnp.concatenate(
        [functools.reduce(jnp.add, [spread[b, j : j + steps] for j in range(0, 8, steps)]) for b in range(rows)],
        axis=0,
    )
    for h in range(heads):
        if h % (heads // 4) == 0:
            vu_copies[h // (heads // 4)].wait()
        mine = jnp.concatenate([sums[b, h * steps : (h + 1) * steps, :] for b in range(rows)], axis=0)
        at = (h % per) * vdim
        part_out[h // per, :, at : at + vdim] = nn_dot(mine.astype(jnp.bfloat16), vu[h]).astype(jnp.bfloat16)
    part_copies, flat_copies = [], []
    for k in range(1, n_ctx):
        target = lax.rem(place + k, n_ctx) if shares > 1 else 0
        for src, dst, send, recv in (
            (stats.at[0], stats.at[k], stat_send, stat_recv),
            (part_out.at[target], part_in.at[k], part_send, part_recv),
        ):
            copy = pltpu.make_async_remote_copy(
                src_ref=src, dst_ref=dst, send_sem=send.at[k], recv_sem=recv.at[k],
                device_id=ctx_peer(k), device_id_type=MESH,
            )
            copy.start()
            part_copies.append(copy)

    fwd_copies = []
    for k in range(1, n_ctx):
        lat_copies[k - 1].wait_recv()
        source = lax.rem(place + n_ctx - k, n_ctx)
        piece = keys.at[pl.ds(pl.multiple_of(source * tokens + role * half, 16), half)]
        for j in range(1, n_role):
            copy = pltpu.make_async_remote_copy(
                src_ref=piece, dst_ref=piece, send_sem=fwd_send.at[k, j], recv_sem=fwd_recv.at[k, j],
                device_id={"role": lax.rem(role + j, n_role)}, device_id_type=MESH,
            )
            copy.start()
            fwd_copies.append(copy)

    for copy in fwd_copies:
        copy.wait_recv()
    seq = n_ctx * tokens
    key_id = lax.broadcasted_iota(jnp.int32, (1, seq), 1)
    key_pos = jnp.zeros((1, seq), jnp.int32)
    for k in range(n_ctx):
        inside = (key_id >= k * tokens) & (key_id < (k + 1) * tokens)
        key_pos = jnp.where(inside, order_ref[k] * tokens + key_id - k * tokens, key_pos)
    query_pos = order_ref[place] * tokens + lax.broadcasted_iota(jnp.int32, (tokens, 1), 0)
    bias = jnp.where(key_pos <= query_pos, 0.0, LOW).astype(jnp.float32)
    group = size["group"]

    for k in range(0, latent, 128):
        keys_t[k : k + 128, :] = keys[:, k : k + 128].T
    keys_t[latent:, :] = keys[:, latent:].T

    def prompt_scores(g):
        block = pl.ds(g * group * tokens, group * tokens)
        return nn_dot(absorbed[block, :latent], keys_t[:latent, :]) + nn_dot(
            absorbed[block, latent:], keys_t[latent:, :]
        )

    prompt_copies = []

    def prompt_finish(g, s):
        s = (s * scale).reshape(group, tokens, seq) + bias[None]
        w = jnp.exp2(s - jnp.max(s, axis=2, keepdims=True))
        inverse = 1.0 / jnp.sum(w, axis=2, keepdims=True)
        o = nn_dot(w.astype(jnp.bfloat16).reshape(group * tokens, seq), keys[:, :latent])
        o = o.astype(jnp.bfloat16)
        for i in range(group):
            h = g * group + i
            head_out = nn_dot(o[i * tokens : (i + 1) * tokens], vu[h]) * inverse[i]
            prompt[:, h * vdim : (h + 1) * vdim] = head_out.astype(jnp.bfloat16)
        cols = slice(g * group * vdim, (g + 1) * group * vdim)
        copy = pltpu.make_async_copy(prompt.at[:, cols], prompt_hbm.at[:, cols], prompt_sem.at[g])
        copy.start()
        prompt_copies.append(copy)

    def merge():
        for copy in part_copies:
            copy.wait_recv()
        peaks = [stats[k, :, :heads] for k in range(n_ctx)]
        top = functools.reduce(jnp.maximum, peaks)
        factors = [jnp.exp2(p - top) for p in peaks]
        whole = functools.reduce(jnp.add, [factors[k] * stats[k, :, 64 : 64 + heads] for k in range(n_ctx)])
        factors = [f / whole for f in factors]
        head_lane = lax.broadcasted_iota(jnp.int32, (made, heads), 1)
        pieces = []
        for j in range(per):
            wanted = head_lane == (place * per + j if shares > 1 else j)
            merged = jnp.zeros((made, vdim), jnp.float32)
            for k in range(n_ctx):
                factor = jnp.sum(jnp.where(wanted, factors[k], 0.0), axis=1, keepdims=True)
                cols = slice(j * vdim, (j + 1) * vdim)
                part = part_in[k, :, cols] if k else part_out[mine_at, :, cols]
                merged = merged + part.astype(jnp.float32) * factor
            pieces.append(merged.astype(jnp.bfloat16))
        in_order = one_hot_rows(made, lambda r: remainder(r, rows) * steps + quotient(r, rows))
        flat[mine_at] = nn_dot(in_order, jnp.concatenate(pieces, axis=1)).astype(jnp.bfloat16)
        for k in range(1, n_ctx if shares > 1 else 1):
            copy = pltpu.make_async_remote_copy(
                src_ref=flat.at[mine_at], dst_ref=flat.at[mine_at], send_sem=flat_send.at[k], recv_sem=flat_recv.at[k],
                device_id=ctx_peer(k), device_id_type=MESH,
            )
            copy.start()
            flat_copies.append(copy)

    n_groups = heads // group
    first = max(n_groups // 2, 1)
    ahead = prompt_scores(0)
    for g in range(first):
        current, ahead = ahead, prompt_scores(g + 1) if g + 1 < n_groups else None
        prompt_finish(g, current)
        if g == 0:
            merge()

    for copy in flat_copies:
        copy.wait_recv()
    for copy in ow_copies:
        copy.wait()
    projected = nn_dot(jnp.concatenate([flat[c] for c in range(shares)], axis=1), ow[...])
    width = projected.shape[1] // plane
    for d in range(plane):
        parts[d] = projected[:, d * width : (d + 1) * width]
    out_copies = []
    for k in range(1, plane):
        copy = pltpu.make_async_remote_copy(
            src_ref=parts.at[lax.rem(here + k, plane)], dst_ref=landed.at[k],
            send_sem=out_send.at[k], recv_sem=out_recv.at[k],
            device_id=plane_peer(k), device_id_type=MESH,
        )
        copy.start()
        out_copies.append(copy)

    for g in range(first, n_groups):
        current, ahead = ahead, prompt_scores(g + 1) if g + 1 < n_groups else None
        prompt_finish(g, current)

    result = parts[here]
    for k in range(1, plane):
        out_copies[k - 1].wait_recv()
        result = result + landed[k]
    step_ref[...] = result
    for copy in lat_copies + fwd_copies + part_copies + flat_copies + out_copies:
        copy.wait_send()
    for copy in prompt_copies:
        copy.wait()


def write_results(prompt_in, step_in, prompt_out, step_out):
    prompt_out[...] = prompt_in[...]
    steps, rows = step_out.shape[:2]
    for t in range(steps):
        step_out[t] = step_in[t * rows : (t + 1) * rows, :].astype(step_out.dtype)


def per_device(
    prompt_query, prompt_latent, block_order, key_up, value_up, out_weight,
    step_query, cache_latent, step_latent, cache_length, block_dest,
):
    tokens, heads, width = prompt_query.shape
    nope, latent = key_up.shape[1:]
    vdim = value_up.shape[2]
    steps, rows = step_query.shape[:2]
    span, key_width = cache_latent.shape[1:]
    model = out_weight.shape[1]
    n_ctx, n_head, n_role = (lax.axis_size(a) for a in ("ctx", "head", "role"))
    plane, made, seq = n_head * n_role, steps * rows, n_ctx * tokens
    shares = n_ctx if heads % n_ctx == 0 else 1
    group = 4 if heads % 4 == 0 and seq <= 512 else 1
    size = dict(
        ctx=n_ctx, head=n_head, role=n_role, tokens=tokens, heads=heads, width=width, nope=nope,
        latent=latent, vdim=vdim, steps=steps, rows=rows, span=span, group=group, shares=shares,
    )
    bf16, f32 = jnp.bfloat16, jnp.float32
    smem, anywhere, vmem = (pl.BlockSpec(memory_space=m) for m in (pltpu.SMEM, pl.ANY, pltpu.VMEM))
    dma = pltpu.SemaphoreType.DMA
    prompt_made, step_made = pl.pallas_call(
        functools.partial(kernel, size),
        out_shape=(
            jax.ShapeDtypeStruct((tokens, heads * vdim), bf16),
            jax.ShapeDtypeStruct((made, model // plane), f32),
        ),
        in_specs=[smem] * 3 + [anywhere] * 7 + [vmem],
        out_specs=(anywhere, vmem),
        scratch_shapes=[
            pltpu.VMEM((tokens * heads, width), bf16),
            pltpu.VMEM(key_up.shape, bf16),
            pltpu.VMEM(value_up.shape, bf16),
            pltpu.VMEM(out_weight.shape, bf16),
            pltpu.VMEM((made * heads, width), bf16),
            pltpu.VMEM((rows, key_width, span), bf16),
            pltpu.VMEM((tokens, key_width), bf16),
            pltpu.VMEM((seq, key_width), bf16),
            pltpu.VMEM((heads, tokens + made, width), bf16),
            pltpu.VMEM((heads * tokens, key_width), bf16),
            pltpu.VMEM((rows, heads * steps, key_width), f32),
            pltpu.VMEM((rows, heads * steps, latent), f32),
            pltpu.VMEM((n_ctx, made, 128), f32),
            pltpu.VMEM((shares, made, heads * vdim // shares), bf16),
            pltpu.VMEM((n_ctx, made, heads * vdim // shares), bf16),
            pltpu.VMEM((shares, made, heads * vdim // shares), bf16),
            pltpu.VMEM((plane, made, model // plane), f32),
            pltpu.VMEM((plane, made, model // plane), f32),
            pltpu.VMEM((tokens, heads * vdim), bf16),
            pltpu.VMEM((key_width, seq), bf16),
            dma((heads // group,)),
            dma((20 + rows,)),
            dma((n_ctx,)), dma((n_ctx,)),
            dma((n_ctx, n_role)), dma((n_ctx, n_role)),
            dma((n_ctx,)), dma((n_ctx,)),
            dma((n_ctx,)), dma((n_ctx,)),
            dma((n_ctx,)), dma((n_ctx,)),
            dma((plane,)), dma((plane,)),
        ],
        compiler_params=pltpu.CompilerParams(
            collective_id=0, has_side_effects=True, vmem_limit_bytes=56 * 1024 * 1024
        ),
    )(
        block_order, cache_length, block_dest,
        prompt_query.reshape(tokens * heads, width), prompt_latent, key_up, value_up, out_weight,
        step_query.reshape(made * heads, width), jnp.swapaxes(cache_latent, 1, 2), step_latent,
    )
    return pl.pallas_call(
        write_results,
        out_shape=(
            jax.ShapeDtypeStruct((tokens, heads * vdim), bf16),
            jax.ShapeDtypeStruct((steps, rows, model // plane), bf16),
        ),
        in_specs=[vmem, vmem],
        out_specs=(vmem, vmem),
        compiler_params=pltpu.CompilerParams(vmem_limit_bytes=56 * 1024 * 1024),
    )(prompt_made, step_made)


def solution(mesh):
    return jax.shard_map(
        per_device,
        mesh=mesh,
        in_specs=(
            P(("groups", "ctx"), ("head", "role"), None),
            P(("groups", "ctx"), None),
            P("groups"),
            P(("head", "role"), None, None),
            P(("head", "role"), None, None),
            P(("head", "role"), "ctx"),
            P(None, "groups", ("head", "role"), None),
            P("groups", "ctx", None),
            P(None, "groups", None),
            P("groups"),
            P("groups"),
        ),
        out_specs=(
            P(("groups", "ctx"), ("head", "role")),
            P(None, "groups", ("ctx", "head", "role")),
        ),
        check_vma=False,
    )
```

```python
import functools
import math

import jax
import jax.numpy as jnp
from jax import lax
from jax.experimental import pallas as pl
from jax.experimental.pallas import tpu as pltpu
from jax.sharding import PartitionSpec as P

MESH = pl.DeviceIdType.MESH
LOW = -1e30


def nt_dot(a, b):
    return lax.dot_general(a, b, (((1,), (1,)), ((), ())), preferred_element_type=jnp.float32)


def nn_dot(a, b):
    return jnp.dot(a, b, preferred_element_type=jnp.float32)


def quotient(x, n):
    return x >> (n.bit_length() - 1) if n & (n - 1) == 0 else lax.div(x, n)


def remainder(x, n):
    return x & (n - 1) if n & (n - 1) == 0 else lax.rem(x, n)


def one_hot_rows(count, source):
    out_row = lax.broadcasted_iota(jnp.int32, (count, count), 0)
    in_row = lax.broadcasted_iota(jnp.int32, (count, count), 1)
    return (in_row == source(out_row)).astype(jnp.bfloat16)


def kernel(
    size,
    order_ref, length_ref, dest_ref,
    pq_hbm, pl_hbm, ku_hbm, vu_hbm, ow_hbm, sq_hbm, cache_hbm, sl_ref,
    prompt_hbm, step_ref,
    pq, ku, vu, ow, sq, cache, own, keys, query, absorbed, step_rows, sums, stats, part_out, part_in, flat, parts, landed,
    prompt, keys_t, prompt_sem, local_sem, lat_send, lat_recv, fwd_send, fwd_recv, part_send, part_recv, stat_send, stat_recv, flat_send, flat_recv, out_send, out_recv,
):
    n_ctx, n_head, n_role = size["ctx"], size["head"], size["role"]
    plane = n_head * n_role
    tokens, heads, nope, latent = size["tokens"], size["heads"], size["nope"], size["latent"]
    steps, rows, span, vdim = size["steps"], size["rows"], size["span"], size["vdim"]
    made = steps * rows
    half = tokens // n_role
    scale = (size["width"] ** -0.5) * math.log2(math.e)
    place, role = lax.axis_index("ctx"), lax.axis_index("role")
    here = lax.axis_index("head") * n_role + role
    shares = size["shares"]
    per = heads // shares
    mine_at = place if shares > 1 else 0

    def ctx_peer(k):
        return {"ctx": lax.rem(place + k, n_ctx)}

    def plane_peer(k):
        other = lax.rem(here + k, plane)
        return {"head": lax.div(other, n_role), "role": lax.rem(other, n_role)}

    started = iter(range(local_sem.shape[0]))

    def load(src, dst, pieces=1):
        copies = []
        step = src.shape[0] // pieces
        for i in range(pieces):
            part = pl.ds(i * step, step)
            copy = pltpu.make_async_copy(src.at[part], dst.at[part], local_sem.at[next(started)])
            copy.start()
            copies.append(copy)
        return copies

    (own_copy,) = load(pl_hbm, own)
    (sq_copy,) = load(sq_hbm, sq)
    pq_copies = load(pq_hbm, pq, 2)
    ku_copies = load(ku_hbm, ku, 4)
    cache_copies = load(cache_hbm, cache, rows)
    vu_copies = load(vu_hbm, vu, 4)
    ow_copies = load(ow_hbm, ow, 8)

    barrier = pltpu.get_barrier_semaphore()
    for k in range(1, n_ctx):
        pl.semaphore_signal(barrier, inc=1, device_id=ctx_peer(k), device_id_type=MESH)
    for k in range(1, plane):
        pl.semaphore_signal(barrier, inc=1, device_id=plane_peer(k), device_id_type=MESH)

    pl.semaphore_wait(barrier, n_ctx - 1 + plane - 1)

    own_copy.wait()
    keys[pl.ds(pl.multiple_of(place * tokens, 16), tokens), :] = own[...]
    my_half = pl.multiple_of(role * half, 16)
    lat_copies = []
    for k in range(1, n_ctx):
        copy = pltpu.make_async_remote_copy(
            src_ref=own.at[pl.ds(my_half, half)],
            dst_ref=keys.at[pl.ds(pl.multiple_of(place * tokens + role * half, 16), half)],
            send_sem=lat_send.at[k], recv_sem=lat_recv.at[k],
            device_id=ctx_peer(k), device_id_type=MESH,
        )
        copy.start()
        lat_copies.append(copy)

    tile = 16

    def prompt_row(r):
        return remainder(r, tile) * heads + quotient(r, tile)

    def step_row(r):
        within = remainder(r, made)
        return (remainder(within, steps) * rows + quotient(within, steps)) * heads + quotient(r, made)

    sq_copy.wait()
    moved = nn_dot(one_hot_rows(made * heads, step_row), sq[...]).astype(jnp.bfloat16)
    query[:, tokens:, :] = moved.reshape(heads, made, size["width"])
    perm = one_hot_rows(tile * heads, prompt_row)
    for copy in pq_copies:
        copy.wait()
    for i in range(tokens // tile):
        moved = nn_dot(perm, pq[i * tile * heads : (i + 1) * tile * heads, :]).astype(jnp.bfloat16)
        query[:, i * tile : (i + 1) * tile, :] = moved.reshape(heads, tile, size["width"])

    for h in range(heads):
        if h % (heads // 4) == 0:
            ku_copies[h // (heads // 4)].wait()
        low = nn_dot(query[h, :, :nope], ku[h]).astype(jnp.bfloat16)
        absorbed[h * tokens : (h + 1) * tokens, :latent] = low[:tokens]
        absorbed[h * tokens : (h + 1) * tokens, latent:] = query[h, :tokens, nope:]
        step_low = low[tokens:].astype(jnp.float32)
        step_high = query[h, tokens:, nope:].astype(jnp.float32)
        for b in range(rows):
            step_rows[b, h * steps : (h + 1) * steps, :latent] = step_low[b * steps : (b + 1) * steps]
            step_rows[b, h * steps : (h + 1) * steps, latent:] = step_high[b * steps : (b + 1) * steps]

    each = heads * steps
    count = rows * each
    row_id = lax.broadcasted_iota(jnp.int32, (count, 1), 0)
    row_step, row_request = remainder(row_id, steps), quotient(row_id, each)
    step_q = step_rows[...].astype(jnp.bfloat16)
    flat_q = step_q.reshape(count, step_q.shape[2])
    fresh = jnp.concatenate([sl_ref[u].astype(jnp.float32) for u in range(steps)], axis=0).astype(jnp.bfloat16)
    fresh_id = lax.broadcasted_iota(jnp.int32, (1, made), 1)
    fresh_mask = (remainder(fresh_id, rows) == row_request) & (quotient(fresh_id, rows) <= row_step) & (place == 0)
    fresh_scores = jnp.where(fresh_mask, nt_dot(flat_q, fresh) * scale, LOW)
    own_scores = jnp.where(row_request == dest_ref[place], nt_dot(flat_q, own[...]) * scale, LOW)
    for copy in cache_copies:
        copy.wait()
    cache_pos = place * span + lax.broadcasted_iota(jnp.int32, (1, span), 1)
    cache_scores = jnp.concatenate(
        [jnp.where(cache_pos < length_ref[b], nn_dot(step_q[b], cache[b]) * scale, LOW) for b in range(rows)], axis=0
    )
    peak = functools.reduce(
        jnp.maximum, [jnp.max(x, axis=1, keepdims=True) for x in (cache_scores, own_scores, fresh_scores)]
    )
    cache_w, own_w, fresh_w = (jnp.exp2(x - peak) for x in (cache_scores, own_scores, fresh_scores))
    amount = functools.reduce(jnp.add, [jnp.sum(x, axis=1, keepdims=True) for x in (cache_w, own_w, fresh_w)])
    cache_w = cache_w.astype(jnp.bfloat16)
    summed = nn_dot(own_w.astype(jnp.bfloat16), own[:, :latent]) + nn_dot(
        fresh_w.astype(jnp.bfloat16), fresh[:, :latent]
    )
    for b in range(rows):
        sums[b] = summed[b * each : (b + 1) * each] + nt_dot(
            cache_w[b * each : (b + 1) * each], cache[b, :latent, :]
        )
    lane = lax.broadcasted_iota(jnp.int32, (1, 128), 1)
    row_head = quotient(remainder(row_id, each), steps)
    spread = jnp.where(lane == row_head, peak, jnp.where(lane == 64 + row_head, amount, 0.0))
    spread = spread.reshape(rows, each // 8, 8, 128).sum(axis=1)
    stats[0] = jnp.concatenate(
        [functools.reduce(jnp.add, [spread[b, j : j + steps] for j in range(0, 8, steps)]) for b in range(rows)],
        axis=0,
    )
    for h in range(heads):
        if h % (heads // 4) == 0:
            vu_copies[h // (heads // 4)].wait()
        mine = jnp.concatenate([sums[b, h * steps : (h + 1) * steps, :] for b in range(rows)], axis=0)
        at = (h % per) * vdim
        part_out[h // per, :, at : at + vdim] = nn_dot(mine.astype(jnp.bfloat16), vu[h]).astype(jnp.bfloat16)
    part_copies, flat_copies = [], []
    for k in range(1, n_ctx):
        target = lax.rem(place + k, n_ctx) if shares > 1 else 0
        for src, dst, send, recv in (
            (stats.at[0], stats.at[k], stat_send, stat_recv),
            (part_out.at[target], part_in.at[k], part_send, part_recv),
        ):
            copy = pltpu.make_async_remote_copy(
                src_ref=src, dst_ref=dst, send_sem=send.at[k], recv_sem=recv.at[k],
                device_id=ctx_peer(k), device_id_type=MESH,
            )
            copy.start()
            part_copies.append(copy)

    fwd_copies = []
    for k in range(1, n_ctx):
        lat_copies[k - 1].wait_recv()
        source = lax.rem(place + n_ctx - k, n_ctx)
        piece = keys.at[pl.ds(pl.multiple_of(source * tokens + role * half, 16), half)]
        for j in range(1, n_role):
            copy = pltpu.make_async_remote_copy(
                src_ref=piece, dst_ref=piece, send_sem=fwd_send.at[k, j], recv_sem=fwd_recv.at[k, j],
                device_id={"role": lax.rem(role + j, n_role)}, device_id_type=MESH,
            )
            copy.start()
            fwd_copies.append(copy)

    for copy in fwd_copies:
        copy.wait_recv()
    seq = n_ctx * tokens
    key_id = lax.broadcasted_iota(jnp.int32, (1, seq), 1)
    key_pos = jnp.zeros((1, seq), jnp.int32)
    for k in range(n_ctx):
        inside = (key_id >= k * tokens) & (key_id < (k + 1) * tokens)
        key_pos = jnp.where(inside, order_ref[k] * tokens + key_id - k * tokens, key_pos)
    query_pos = order_ref[place] * tokens + lax.broadcasted_iota(jnp.int32, (tokens, 1), 0)
    bias = jnp.where(key_pos <= query_pos, 0.0, LOW).astype(jnp.float32)
    group = size["group"]

    for k in range(0, latent, 128):
        keys_t[k : k + 128, :] = keys[:, k : k + 128].T
    keys_t[latent:, :] = keys[:, latent:].T

    def prompt_scores(g):
        block = pl.ds(g * group * tokens, group * tokens)
        return nn_dot(absorbed[block, :latent], keys_t[:latent, :]) + nn_dot(
            absorbed[block, latent:], keys_t[latent:, :]
        )

    prompt_copies = []

    def prompt_finish(g, s):
        s = (s * scale).reshape(group, tokens, seq) + bias[None]
        w = jnp.exp2(s - jnp.max(s, axis=2, keepdims=True))
        inverse = 1.0 / jnp.sum(w, axis=2, keepdims=True)
        o = nn_dot(w.astype(jnp.bfloat16).reshape(group * tokens, seq), keys[:, :latent])
        o = o.astype(jnp.bfloat16)
        for i in range(group):
            h = g * group + i
            head_out = nn_dot(o[i * tokens : (i + 1) * tokens], vu[h]) * inverse[i]
            prompt[:, h * vdim : (h + 1) * vdim] = head_out.astype(jnp.bfloat16)
        cols = slice(g * group * vdim, (g + 1) * group * vdim)
        copy = pltpu.make_async_copy(prompt.at[:, cols], prompt_hbm.at[:, cols], prompt_sem.at[g])
        copy.start()
        prompt_copies.append(copy)

    def merge():
        for copy in part_copies:
            copy.wait_recv()
        peaks = [stats[k, :, :heads] for k in range(n_ctx)]
        top = functools.reduce(jnp.maximum, peaks)
        factors = [jnp.exp2(p - top) for p in peaks]
        whole = functools.reduce(jnp.add, [factors[k] * stats[k, :, 64 : 64 + heads] for k in range(n_ctx)])
        factors = [f / whole for f in factors]
        head_lane = lax.broadcasted_iota(jnp.int32, (made, heads), 1)
        pieces = []
        for j in range(per):
            wanted = head_lane == (place * per + j if shares > 1 else j)
            merged = jnp.zeros((made, vdim), jnp.float32)
            for k in range(n_ctx):
                factor = jnp.sum(jnp.where(wanted, factors[k], 0.0), axis=1, keepdims=True)
                cols = slice(j * vdim, (j + 1) * vdim)
                part = part_in[k, :, cols] if k else part_out[mine_at, :, cols]
                merged = merged + part.astype(jnp.float32) * factor
            pieces.append(merged.astype(jnp.bfloat16))
        in_order = one_hot_rows(made, lambda r: remainder(r, rows) * steps + quotient(r, rows))
        flat[mine_at] = nn_dot(in_order, jnp.concatenate(pieces, axis=1)).astype(jnp.bfloat16)
        for k in range(1, n_ctx if shares > 1 else 1):
            copy = pltpu.make_async_remote_copy(
                src_ref=flat.at[mine_at], dst_ref=flat.at[mine_at], send_sem=flat_send.at[k], recv_sem=flat_recv.at[k],
                device_id=ctx_peer(k), device_id_type=MESH,
            )
            copy.start()
            flat_copies.append(copy)

    n_groups = heads // group
    first = max(n_groups - 1, 1)
    ahead = prompt_scores(0)
    for g in range(first):
        current, ahead = ahead, prompt_scores(g + 1) if g + 1 < n_groups else None
        prompt_finish(g, current)
        if g == 0:
            merge()

    for copy in flat_copies:
        copy.wait_recv()
    for copy in ow_copies:
        copy.wait()
    projected = nn_dot(jnp.concatenate([flat[c] for c in range(shares)], axis=1), ow[...])
    width = projected.shape[1] // plane
    for d in range(plane):
        parts[d] = projected[:, d * width : (d + 1) * width]
    out_copies = []
    for k in range(1, plane):
        copy = pltpu.make_async_remote_copy(
            src_ref=parts.at[lax.rem(here + k, plane)], dst_ref=landed.at[k],
            send_sem=out_send.at[k], recv_sem=out_recv.at[k],
            device_id=plane_peer(k), device_id_type=MESH,
        )
        copy.start()
        out_copies.append(copy)

    for g in range(first, n_groups):
        current, ahead = ahead, prompt_scores(g + 1) if g + 1 < n_groups else None
        prompt_finish(g, current)

    result = parts[here]
    for k in range(1, plane):
        out_copies[k - 1].wait_recv()
        result = result + landed[k]
    step_ref[...] = result
    for copy in lat_copies + fwd_copies + part_copies + flat_copies + out_copies:
        copy.wait_send()
    for copy in prompt_copies:
        copy.wait()


def write_results(prompt_in, step_in, prompt_out, step_out):
    prompt_out[...] = prompt_in[...]
    steps, rows = step_out.shape[:2]
    for t in range(steps):
        step_out[t] = step_in[t * rows : (t + 1) * rows, :].astype(step_out.dtype)


def per_device(
    prompt_query, prompt_latent, block_order, key_up, value_up, out_weight,
    step_query, cache_latent, step_latent, cache_length, block_dest,
):
    tokens, heads, width = prompt_query.shape
    nope, latent = key_up.shape[1:]
    vdim = value_up.shape[2]
    steps, rows = step_query.shape[:2]
    span, key_width = cache_latent.shape[1:]
    model = out_weight.shape[1]
    n_ctx, n_head, n_role = (lax.axis_size(a) for a in ("ctx", "head", "role"))
    plane, made, seq = n_head * n_role, steps * rows, n_ctx * tokens
    shares = n_ctx if heads % n_ctx == 0 else 1
    group = 4 if heads % 4 == 0 and seq <= 512 else 1
    size = dict(
        ctx=n_ctx, head=n_head, role=n_role, tokens=tokens, heads=heads, width=width, nope=nope,
        latent=latent, vdim=vdim, steps=steps, rows=rows, span=span, group=group, shares=shares,
    )
    bf16, f32 = jnp.bfloat16, jnp.float32
    smem, anywhere, vmem = (pl.BlockSpec(memory_space=m) for m in (pltpu.SMEM, pl.ANY, pltpu.VMEM))
    dma = pltpu.SemaphoreType.DMA
    prompt_made, step_made = pl.pallas_call(
        functools.partial(kernel, size),
        out_shape=(
            jax.ShapeDtypeStruct((tokens, heads * vdim), bf16),
            jax.ShapeDtypeStruct((made, model // plane), f32),
        ),
        in_specs=[smem] * 3 + [anywhere] * 7 + [vmem],
        out_specs=(anywhere, vmem),
        scratch_shapes=[
            pltpu.VMEM((tokens * heads, width), bf16),
            pltpu.VMEM(key_up.shape, bf16),
            pltpu.VMEM(value_up.shape, bf16),
            pltpu.VMEM(out_weight.shape, bf16),
            pltpu.VMEM((made * heads, width), bf16),
            pltpu.VMEM((rows, key_width, span), bf16),
            pltpu.VMEM((tokens, key_width), bf16),
            pltpu.VMEM((seq, key_width), bf16),
            pltpu.VMEM((heads, tokens + made, width), bf16),
            pltpu.VMEM((heads * tokens, key_width), bf16),
            pltpu.VMEM((rows, heads * steps, key_width), f32),
            pltpu.VMEM((rows, heads * steps, latent), f32),
            pltpu.VMEM((n_ctx, made, 128), f32),
            pltpu.VMEM((shares, made, heads * vdim // shares), bf16),
            pltpu.VMEM((n_ctx, made, heads * vdim // shares), bf16),
            pltpu.VMEM((shares, made, heads * vdim // shares), bf16),
            pltpu.VMEM((plane, made, model // plane), f32),
            pltpu.VMEM((plane, made, model // plane), f32),
            pltpu.VMEM((tokens, heads * vdim), bf16),
            pltpu.VMEM((key_width, seq), bf16),
            dma((heads // group,)),
            dma((20 + rows,)),
            dma((n_ctx,)), dma((n_ctx,)),
            dma((n_ctx, n_role)), dma((n_ctx, n_role)),
            dma((n_ctx,)), dma((n_ctx,)),
            dma((n_ctx,)), dma((n_ctx,)),
            dma((n_ctx,)), dma((n_ctx,)),
            dma((plane,)), dma((plane,)),
        ],
        compiler_params=pltpu.CompilerParams(
            collective_id=0, has_side_effects=True, vmem_limit_bytes=56 * 1024 * 1024
        ),
    )(
        block_order, cache_length, block_dest,
        prompt_query.reshape(tokens * heads, width), prompt_latent, key_up, value_up, out_weight,
        step_query.reshape(made * heads, width), jnp.swapaxes(cache_latent, 1, 2), step_latent,
    )
    return pl.pallas_call(
        write_results,
        out_shape=(
            jax.ShapeDtypeStruct((tokens, heads * vdim), bf16),
            jax.ShapeDtypeStruct((steps, rows, model // plane), bf16),
        ),
        in_specs=[vmem, vmem],
        out_specs=(vmem, vmem),
        compiler_params=pltpu.CompilerParams(vmem_limit_bytes=56 * 1024 * 1024),
    )(prompt_made, step_made)


def solution(mesh):
    return jax.shard_map(
        per_device,
        mesh=mesh,
        in_specs=(
            P(("groups", "ctx"), ("head", "role"), None),
            P(("groups", "ctx"), None),
            P("groups"),
            P(("head", "role"), None, None),
            P(("head", "role"), None, None),
            P(("head", "role"), "ctx"),
            P(None, "groups", ("head", "role"), None),
            P("groups", "ctx", None),
            P(None, "groups", None),
            P("groups"),
            P("groups"),
        ),
        out_specs=(
            P(("groups", "ctx"), ("head", "role")),
            P(None, "groups", ("ctx", "head", "role")),
        ),
        check_vma=False,
    )
```
